128 devices in a mesh: outer: 8 (over z, x_hi), inner: 16 (over y, x_lo, core).
Axes of the slice: x: 4 (x_hi: 2, x_lo: 2; x = x_hi * 2 + x_lo), y: 4, z: 4, core: 2. Of those that a mesh axis runs over, the one named last changes fastest.
Arguments:
- queries: bfloat16 [16384, 3072], P(('outer', 'inner')), may hold values from -16 to 16
- keys: bfloat16 [16384, 512], P(('outer', 'inner')), may hold values from -16 to 16
- values: bfloat16 [16384, 512], P(('outer', 'inner')), may hold values from -6 to 6
- output_gradient: bfloat16 [16384, 3072], P(('outer', 'inner')), may hold values from -6 to 6
- span_order: int32 [32], replicated, may hold values from 0 to 31, each once
Outputs:
- grad_queries: bfloat16 [16384, 3072], P(('outer', 'inner'))
- key_gradients_out: bfloat16 [16384, 512], P(('outer', 'inner'))
- value_gradients_out: bfloat16 [16384, 512], P(('outer', 'inner'))
The draws below stay inside these ranges and needn't reach their ends.
Inputs may be any that keep to these rules, and one draw needn't show every extreme that they name: `span_order`: each of 0 to 31 once.
All inputs are finite; a program needn't handle non-finite values.
Results may differ from the reference program's by a relative error of at most 0.04.
Values may be sent and summed in bfloat16 or wider, within the bound.
A program may use at most 128 MiB of HBM per device.

```python
from functools import partial
import jax
import jax.numpy as jnp
from jax import lax

QUERY_HEADS = 24
KEY_HEADS = 4
HEAD_SIZE = 128
QUERIES_PER_KEY = 6
HALF = 64
SPANS = 32
GROUP_TOKENS = 2048
SEQUENCE_TOKENS = 16384
N_OUTER = 8


def draw_queries(key, part):
    key = jax.random.fold_in(key, 1)
    final_result = jnp.clip(jax.random.normal(key, (SEQUENCE_TOKENS, QUERY_HEADS * HEAD_SIZE), jnp.float32), -4.5, 4.5)
    return final_result.astype(jnp.bfloat16)


def draw_keys(key, part):
    key = jax.random.fold_in(key, 2)
    final_result = jnp.clip(jax.random.normal(key, (SEQUENCE_TOKENS, KEY_HEADS * HEAD_SIZE), jnp.float32), -4.5, 4.5)
    return final_result.astype(jnp.bfloat16)


def level_of(rng, shape, cuts, smallest, high):
    def one(dim, blocks):
        steps = jax.random.uniform(jax.random.fold_in(jax.random.fold_in(rng, 6), dim), (blocks,), jnp.float32, smallest / len(cuts), high / len(cuts))
        return jnp.repeat(jnp.exp(steps), shape[dim] // blocks).reshape((-1,) + (1,) * (len(shape) - dim - 1))

    loudness = one(*cuts[0])
    for cut in cuts[1:]:
        loudness = loudness * one(*cut)
    return loudness


def normal_values(rng, shape, deviation, most, pieces=(), kind=jnp.bfloat16):
    loudness = level_of(rng, shape, pieces, -0.22, 0.18) if pieces else 1.0
    entries = jax.random.normal(rng, shape, jnp.float32) * deviation * loudness
    return jnp.minimum(jnp.maximum(entries, -most), most).astype(kind)


def setup_inputs(seed: int = 0) -> dict:
    key_of = jax.random.split(jax.random.key(seed), 6)
    return {
        "queries": draw_queries(jax.random.fold_in(key_of[5], 71), 0),
        "keys": draw_keys(jax.random.fold_in(key_of[5], 71), 0),
        "values": normal_values(key_of[2], (SEQUENCE_TOKENS, KEY_HEADS * HEAD_SIZE), 1.0, 6.0, ((0, 128),)),
        "output_gradient": normal_values(key_of[3], (SEQUENCE_TOKENS, QUERY_HEADS * HEAD_SIZE), 1.0, 6.0, ((0, 128),)),
        "span_order": jax.random.permutation(key_of[4], SPANS).astype(jnp.int32),
    }


masked_score = -1.0e30


def group_positions(span_order):
    within = jnp.arange(GROUP_TOKENS, dtype=jnp.int32)
    return span_order[within // HALF] * HALF + within % HALF


def head_grads(visible, scale, operands):
    query_head, key_head, value_head, grad_head = operands
    query_f32 = query_head.astype(jnp.float32)
    key_f32 = key_head.astype(jnp.float32)
    value_f32 = value_head.astype(jnp.float32)
    grad_f32 = grad_head.astype(jnp.float32)
    scores = jnp.einsum("agd,jd->agj", query_f32, key_f32) * scale
    scores = jnp.where(visible, scores, masked_score)
    top_score = jnp.max(scores, axis=-1, keepdims=True)
    total = jnp.sum(jnp.where(visible, jnp.exp(scores - top_score), 0.0), axis=-1, keepdims=True)
    log_total = top_score + jnp.log(total)
    probabilities = jnp.where(visible, jnp.exp(scores - log_total), 0.0)
    probs_low = probabilities.astype(jnp.bfloat16).astype(jnp.float32)
    output = jnp.einsum("agj,jd->agd", probs_low, value_f32).astype(jnp.bfloat16).astype(jnp.float32)
    delta = jnp.sum(grad_f32 * output, axis=-1, keepdims=True)
    grad_value = jnp.einsum("agj,agd->jd", probs_low, grad_f32)
    dprobs = jnp.einsum("agd,jd->agj", grad_f32, value_f32)
    score_gradient = (probabilities * (dprobs - delta)).astype(jnp.bfloat16).astype(jnp.float32)
    grad_query = jnp.einsum("agj,jd->agd", score_gradient, key_f32) * scale
    grad_key = jnp.einsum("agj,agd->jd", score_gradient, query_f32) * scale
    return grad_query, grad_key, grad_value


def reference(queries, keys, values, output_gradient, span_order):
    scale = HEAD_SIZE ** -0.5
    inpos = group_positions(span_order)
    causal = inpos[None, :] <= inpos[:, None]
    query_pieces = []
    key_gradients_out = jnp.zeros((SEQUENCE_TOKENS, KEY_HEADS * HEAD_SIZE), jnp.float32)
    value_gradients_out = jnp.zeros((SEQUENCE_TOKENS, KEY_HEADS * HEAD_SIZE), jnp.float32)
    for outer_idx in range(N_OUTER):
        lower_bound = outer_idx * GROUP_TOKENS
        upper_bound = lower_bound + GROUP_TOKENS
        current_keys = keys[lower_bound:upper_bound]
        current_values = values[lower_bound:upper_bound]
        if outer_idx > 0:
            earlier_keys = keys[lower_bound - GROUP_TOKENS:lower_bound]
            earlier_values = values[lower_bound - GROUP_TOKENS:lower_bound]
        else:
            earlier_keys = jnp.zeros_like(current_keys)
            earlier_values = jnp.zeros_like(current_values)
        visible = jnp.concatenate([jnp.full((GROUP_TOKENS, GROUP_TOKENS), outer_idx > 0), causal], axis=1)
        stacked_keys = jnp.concatenate([earlier_keys, current_keys], axis=0).reshape(2 * GROUP_TOKENS, KEY_HEADS, HEAD_SIZE).transpose(1, 0, 2)
        stacked_values = jnp.concatenate([earlier_values, current_values], axis=0).reshape(2 * GROUP_TOKENS, KEY_HEADS, HEAD_SIZE).transpose(1, 0, 2)
        stacked_queries = queries[lower_bound:upper_bound].reshape(GROUP_TOKENS, KEY_HEADS, QUERIES_PER_KEY, HEAD_SIZE).transpose(1, 2, 0, 3)
        gradient_stack = output_gradient[lower_bound:upper_bound].reshape(GROUP_TOKENS, KEY_HEADS, QUERIES_PER_KEY, HEAD_SIZE).transpose(1, 2, 0, 3)
        query_gradient, key_gradient, value_gradient = lax.map(partial(head_grads, visible, scale), (stacked_queries, stacked_keys, stacked_values, gradient_stack))
        query_pieces.append(query_gradient.transpose(2, 0, 1, 3).reshape(GROUP_TOKENS, KEY_HEADS * QUERIES_PER_KEY * HEAD_SIZE))
        rows_of_keys = key_gradient.transpose(1, 0, 2).reshape(2 * GROUP_TOKENS, KEY_HEADS * HEAD_SIZE)
        rows_of_values = value_gradient.transpose(1, 0, 2).reshape(2 * GROUP_TOKENS, KEY_HEADS * HEAD_SIZE)
        if outer_idx > 0:
            key_gradients_out = key_gradients_out.at[lower_bound - GROUP_TOKENS:lower_bound].add(rows_of_keys[:GROUP_TOKENS])
            value_gradients_out = value_gradients_out.at[lower_bound - GROUP_TOKENS:lower_bound].add(rows_of_values[:GROUP_TOKENS])
        key_gradients_out = key_gradients_out.at[lower_bound:upper_bound].add(rows_of_keys[GROUP_TOKENS:])
        value_gradients_out = value_gradients_out.at[lower_bound:upper_bound].add(rows_of_values[GROUP_TOKENS:])
    grad_queries = jnp.concatenate(query_pieces, axis=0).astype(jnp.bfloat16)
    return (grad_queries, key_gradients_out.astype(jnp.bfloat16), value_gradients_out.astype(jnp.bfloat16))
```

```python
import jax
import jax.numpy as jnp
from jax import lax
from jax.experimental import pallas as pl
from jax.experimental.pallas import tpu as pltpu
from jax.sharding import PartitionSpec as P

MESH = pl.DeviceIdType.MESH
F32 = jnp.float32
BF16 = jnp.bfloat16
SCALE = 128**-0.5
SCALE2 = SCALE * 1.4426950408889634
MASKED = -1.0e30
NT = (((1,), (1,)), ((), ()))

HEAD = 128
TOK = 128
NH = 3
SET = 2 * TOK
ROWS = NH * SET
COLS = NH * HEAD
SEG = 8 * TOK
NKEY = 4 * SEG
BK = SEG
VR = 16


def kernel(
    q_ref, k_ref, v_ref, do_ref, span_ref,
    gq_ref, gk_ref, gv_ref,
    qraw, doraw, kvg, pk, pq, qt, dot, s_buf, dp_buf, e_buf, mx, ls, dd, dqa, dka, dva, dqs,
    cx, rx, xs, xr, ys, yr,
    q_ssem, q_rsem, y_ssem, y_rsem, x_ssem, x_rsem, c_ssem, c_rsem, l_sem,
    dq_ssem, dq_rsem, rc_ssem, rc_rsem, rx_ssem, rx_rsem, ry_ssem, ry_rsem,
):
    o = lax.axis_index("outer")
    i = lax.axis_index("inner")
    y, xl, c = i // 4, (i // 2) % 2, i % 2
    has_prev = o > 0
    has_next = o < 7

    def dev(oo, yy, xx, cc):
        return (oo, yy * 4 + xx * 2 + cc)

    def yrel(d):
        return lax.rem(y + d, 4)

    def remote(src, dst, ssem, rsem, device):
        return pltpu.make_async_remote_copy(
            src_ref=src, dst_ref=dst, send_sem=ssem, recv_sem=rsem, device_id=device, device_id_type=MESH
        )

    o_next, o_prev = lax.rem(o + 1, 8), lax.rem(o + 7, 8)
    core = dev(o, y, xl, 1 - c)

    barrier = pltpu.get_barrier_semaphore()
    peers = [dev(o, yrel(d), xl, cc) for d in range(1, 4) for cc in range(2)]
    peers += [core, dev(o, y, 1 - xl, c)]
    peers += [dev(oo, y, xx, c) for oo in (o_next, o_prev) for xx in range(2)]
    for p in peers:
        pl.semaphore_signal(barrier, inc=1, device_id=p, device_id_type=MESH)
    pl.semaphore_wait(barrier, len(peers))

    def rows(seg, cc, yy=0, n=4):
        return pl.ds(pl.multiple_of(seg * SEG + cc * 4 * TOK + yy * TOK, TOK), n * TOK)

    def kv_copy(t, d):
        yy = yrel(d)
        src = (k_ref, v_ref)[t].at[:, pl.ds(pl.multiple_of(yy * HEAD, HEAD), HEAD)]
        return remote(src, kvg.at[t, rows(0, c, y, 1)], y_ssem.at[t, d - 1], y_rsem.at[t, 3 - d], dev(o, yy, xl, c))

    def kv_local(t):
        src = (k_ref, v_ref)[t].at[:, pl.ds(pl.multiple_of(y * HEAD, HEAD), HEAD)]
        return pltpu.make_async_copy(src, kvg.at[t, rows(0, c, y, 1)], l_sem.at[t])

    def q_copy(t, d, dc):
        yy, cc = yrel(d), (1 - c if dc else c)
        src = (q_ref, do_ref)[t].at[:, pl.ds(pl.multiple_of((yy * 2 + cc) * COLS, 128), COLS)]
        dst = (qraw, doraw)[t].at[(4 - d) % 4, pl.ds(pl.multiple_of(c * TOK, TOK), TOK)]
        r = (4 - d) % 4
        return remote(src, dst, q_ssem.at[t, d, dc], q_rsem.at[t, r, dc], dev(o, yy, xl, cc))

    def q_local(t):
        src = (q_ref, do_ref)[t].at[:, pl.ds(pl.multiple_of((y * 2 + c) * COLS, 128), COLS)]
        dst = (qraw, doraw)[t].at[0, pl.ds(pl.multiple_of(c * TOK, TOK), TOK)]
        return pltpu.make_async_copy(src, dst, l_sem.at[2 + t])

    def x_copy(n):
        src = kvg.at[:, rows(0, c)]
        if n == 0:
            return remote(src, kvg.at[:, rows(1, c)], x_ssem.at[0], x_rsem.at[0], dev(o, y, 1 - xl, c))
        return remote(src, kvg.at[:, rows(2 + xl, c)], x_ssem.at[n], x_rsem.at[1 + xl], dev(o_next, y, n - 1, c))

    def x_arrival(n):
        dst = kvg.at[:, rows(1 + n, c)]
        return remote(dst, dst, x_ssem.at[0], x_rsem.at[n], core)

    def c_copy(seg):
        blk = kvg.at[:, rows(seg, c)]
        return remote(blk, blk, c_ssem.at[seg], c_rsem.at[seg], core)

    def c_arrival(seg):
        blk = kvg.at[:, rows(seg, 1 - c)]
        return remote(blk, blk, c_ssem.at[seg], c_rsem.at[seg], core)

    for t in range(2):
        kv_local(t).start()
        q_local(t).start()
        for d in range(1, 4):
            kv_copy(t, d).start()
    for d in (0, 3, 1, 2):
        for dc in range(2):
            for t in range(2):
                if d or dc:
                    q_copy(t, d, dc).start()

    def pk_row(blk, value):
        pk[:, pl.ds(pl.multiple_of(blk * TOK, TOK), TOK)] = value

    lane = lax.broadcasted_iota(jnp.int32, (8, TOK), 1)
    for xx in range(2):
        for cc in range(2):
            for yy in range(4):
                first = 2 * (yy * 4 + xx * 2 + cc)
                span = jnp.where(lane < 64, span_ref[first], span_ref[first + 1])
                blk = jnp.where(xl == xx, 0, 8) + cc * 4 + yy
                pk_row(blk, (span * 64 + lax.rem(lane, 64)).astype(F32))
    for blk in range(16, 32):
        pk_row(blk, jnp.full((8, TOK), -1.0, F32))
    sub = lax.broadcasted_iota(jnp.int32, (64, 128), 0)
    for rel in range(4):
        for cc in range(2):
            for hb in range(2):
                span = span_ref[2 * (yrel(rel) * 4 + xl * 2 + cc) + hb]
                at = (cc * 2 + hb) * 64
                pq[rel, at : at + 64, :] = (span * 64 + sub).astype(F32)

    dka[...] = jnp.zeros_like(dka)
    dva[...] = jnp.zeros_like(dva)

    for t in range(2):
        kv_local(t).wait()
        for d in range(1, 4):
            kv_copy(t, d).wait_recv()
    x_copy(0).start()

    @pl.when(has_next)
    def _():
        x_copy(1).start()
        x_copy(2).start()

    c_copy(0).start()
    c_arrival(0).wait_recv()
    x_arrival(0).wait_recv()
    c_copy(1).start()

    @pl.when(has_prev)
    def _():
        for n in (1, 2):
            x_arrival(n).wait_recv()
            c_copy(1 + n).start()

    c_arrival(1).wait_recv()

    @pl.when(has_prev)
    def _():
        c_arrival(2).wait_recv()
        c_arrival(3).wait_recv()

    for t in range(2):
        q_local(t).wait()
    for r in range(4):
        for dc in range(2):
            for t in range(2):
                if r or dc:
                    q_copy(t, (4 - r) % 4, dc).wait_recv()

    nblk = jnp.where(has_prev, 4, 2)

    def lanes(b, j):
        return pl.ds(pl.multiple_of(b * BK + j * 128, 128), 128)

    def row_set(rel, _):
        mx[...] = jnp.full(mx.shape, MASKED, F32)

        def scores(b, _):
            keys = kvg[0, pl.ds(pl.multiple_of(b * BK, BK), BK), :]
            for h in range(NH):
                r = slice(h * SET, h * SET + SET)
                s = lax.dot_general(
                    qraw[rel, :, h * HEAD : h * HEAD + HEAD], keys, NT, preferred_element_type=F32
                )
                m = mx[r, :]
                for j in range(BK // 128):
                    sj = jnp.where(pk[0:1, lanes(b, j)] <= pq[rel], s[:, j * 128 : j * 128 + 128], MASKED)
                    m = jnp.maximum(m, sj)
                    s_buf[r, lanes(b, j)] = sj
                mx[r, :] = m
            return 0

        lax.fori_loop(0, nblk, scores, 0)
        for h in range(NH):
            r = slice(h * SET, h * SET + SET)
            mx[r, :] = jnp.broadcast_to(jnp.max(mx[r, :], axis=1, keepdims=True) * SCALE2, (SET, 128))
        ls[...] = jnp.zeros_like(ls)
        dd[...] = jnp.zeros_like(dd)

        def weights(b, _):
            vals = kvg[1, pl.ds(pl.multiple_of(b * BK, BK), BK), :]
            for h in range(NH):
                dp = lax.dot_general(
                    doraw[rel, :, h * HEAD : h * HEAD + HEAD], vals, NT, preferred_element_type=F32
                )
                for g0 in range(0, SET, VR):
                    g = slice(h * SET + g0, h * SET + g0 + VR)
                    m, l, d = mx[g, :], ls[g, :], dd[g, :]
                    for j in range(BK // 128):
                        e = jnp.exp2(s_buf[g, lanes(b, j)] * SCALE2 - m)
                        dpj = dp[g0 : g0 + VR, j * 128 : j * 128 + 128]
                        l = l + e
                        d = d + e * dpj
                        e_buf[g, lanes(b, j)] = e.astype(BF16)
                        dp_buf[g, lanes(b, j)] = dpj
                    ls[g, :] = l
                    dd[g, :] = d
            return 0

        lax.fori_loop(0, nblk, weights, 0)
        for h in range(NH):
            r = slice(h * SET, h * SET + SET)
            rinv = 1.0 / jnp.sum(ls[r, :], axis=1, keepdims=True)
            delta = jnp.sum(dd[r, :], axis=1, keepdims=True) * rinv
            ls[r, :] = jnp.broadcast_to(rinv, (SET, 128))
            dd[r, :] = jnp.broadcast_to(delta, (SET, 128))
            hc = slice(h * HEAD, h * HEAD + HEAD)
            qt[:, r] = (qraw[rel, :, hc].astype(F32) * rinv).astype(BF16).T
            dot[:, r] = (doraw[rel, :, hc].astype(F32) * rinv).astype(BF16).T
        dqa[...] = jnp.zeros_like(dqa)

        def grads(b, _):
            at = pl.ds(pl.multiple_of(b * BK, BK), BK)
            keys = kvg[0, at, :]
            dv = jnp.dot(dot[...], e_buf[:, at], preferred_element_type=F32)
            dk = None
            for h in range(NH):
                r = slice(h * SET, h * SET + SET)
                parts = []
                for g0 in range(0, SET, VR):
                    g = slice(h * SET + g0, h * SET + g0 + VR)
                    d = dd[g, :]
                    parts.append(
                        jnp.concatenate(
                            [
                                (e_buf[g, lanes(b, j)].astype(F32) * (dp_buf[g, lanes(b, j)] - d)).astype(BF16)
                                for j in range(BK // 128)
                            ],
                            axis=1,
                        )
                    )
                ds = jnp.concatenate(parts, axis=0)
                dqa[r, :] += jnp.dot(ds, keys, preferred_element_type=F32)
                part = jnp.dot(qt[:, r], ds, preferred_element_type=F32)
                dk = part if dk is None else dk + part
            for j in range(BK // 128):
                blk = b * (BK // 128) + j
                dva[blk] += dv[:, j * 128 : j * 128 + 128]
                dka[blk] += dk[:, j * 128 : j * 128 + 128]
            return 0

        lax.fori_loop(0, nblk, grads, 0)
        for h in range(NH):
            r = slice(h * SET, h * SET + SET)
            dqs[rel, :, h * HEAD : h * HEAD + HEAD] = (dqa[r, :] * (ls[r, :] * SCALE)).astype(BF16)
        return 0

    lax.fori_loop(0, 4, row_set, 0)

    mine = pl.ds(pl.multiple_of((y * 2 + c) * COLS, 128), COLS)

    def dq_copy(r, dc):
        cc = 1 - c if dc else c
        src = dqs.at[r, pl.ds(pl.multiple_of(cc * TOK, TOK), TOK)]
        return remote(
            src, gq_ref.at[:, mine], dq_ssem.at[r, dc], dq_rsem.at[(4 - r) % 4, dc], dev(o, yrel(r), xl, cc)
        )

    def dq_arrival(r, dc):
        cc = 1 - c if dc else c
        dst = gq_ref.at[:, pl.ds(pl.multiple_of((yrel(r) * 2 + cc) * COLS, 128), COLS)]
        return remote(dst, dst, dq_ssem.at[0, 1], dq_rsem.at[r, dc], core)

    for r in range(4):
        for dc in range(2):
            if r or dc:
                dq_copy(r, dc).start()
    dq_local = pltpu.make_async_copy(
        dqs.at[0, pl.ds(pl.multiple_of(c * TOK, TOK), TOK)], gq_ref.at[:, mine], l_sem.at[4]
    )
    dq_local.start()

    acc = (dka, dva)

    def rc_copy(seg):
        return remote(cx.at[seg], rx.at[seg], rc_ssem.at[seg], rc_rsem.at[seg], core)

    def rx_copy(n):
        if n == 0:
            return remote(xs.at[0], xr.at[0], rx_ssem.at[0], rx_rsem.at[0], dev(o, y, 1 - xl, c))
        return remote(xs.at[n], xr.at[1 + xl], rx_ssem.at[n], rx_rsem.at[1 + xl], dev(o_prev, y, n - 1, c))

    def rx_arrival(n):
        return remote(xr.at[n], xr.at[n], rx_ssem.at[0], rx_rsem.at[n], core)

    def ry_copy(d):
        yy = yrel(d)
        return remote(ys.at[yy], yr.at[y], ry_ssem.at[d - 1], ry_rsem.at[3 - d], dev(o, yy, xl, c))

    def ry_arrival(r):
        dst = yr.at[yrel(r)]
        return remote(dst, dst, ry_ssem.at[0], ry_rsem.at[r - 1], core)

    def send_core(seg):
        def step(yy, _):
            for t in range(2):
                cx[seg, t, yy] = acc[t][seg * 8 + (1 - c) * 4 + yy].astype(BF16)
            return 0

        lax.fori_loop(0, 4, step, 0)
        rc_copy(seg).start()

    def send_x(seg):
        rc_copy(seg).wait_recv()

        def step(yy, _):
            for t in range(2):
                xs[seg - 1, t, yy] = (acc[t][seg * 8 + c * 4 + yy] + rx[seg, t, yy].astype(F32)).astype(BF16)
            return 0

        lax.fori_loop(0, 4, step, 0)
        rx_copy(seg - 1).start()

    @pl.when(has_prev)
    def _():
        send_core(2)
        send_core(3)

    send_core(1)
    send_core(0)

    @pl.when(has_prev)
    def _():
        send_x(2)
        send_x(3)

    send_x(1)
    rc_copy(0).wait_recv()

    def own(yy, _):
        for t in range(2):
            blk = c * 4 + yy
            acc[t][blk] = acc[t][blk] + rx[0, t, yy].astype(F32)
        return 0

    lax.fori_loop(0, 4, own, 0)

    def take(n):
        rx_arrival(n).wait_recv()

        def step(yy, _):
            for t in range(2):
                blk = c * 4 + yy
                acc[t][blk] = acc[t][blk] + xr[n, t, yy].astype(F32)
            return 0

        lax.fori_loop(0, 4, step, 0)

    take(0)

    @pl.when(has_next)
    def _():
        take(1)
        take(2)

    def final(yy, _):
        blk = c * 4 + yy
        ys[yy, 0] = (acc[0][blk] * SCALE).astype(BF16)
        ys[yy, 1] = acc[1][blk].astype(BF16)
        return 0

    lax.fori_loop(0, 4, final, 0)
    for d in range(1, 4):
        ry_copy(d).start()
    outs = (gk_ref, gv_ref)
    at_me = pl.ds(pl.multiple_of(y * HEAD, HEAD), HEAD)
    for t in range(2):
        outs[t][:, at_me] = ys[y, t].T
    for r in range(1, 4):
        ry_arrival(r).wait_recv()
        at = pl.ds(pl.multiple_of(yrel(r) * HEAD, HEAD), HEAD)
        for t in range(2):
            outs[t][:, at] = yr[yrel(r), t].T

    dq_local.wait()
    for r in range(4):
        for dc in range(2):
            if r or dc:
                dq_arrival(r, dc).wait_recv()
                dq_copy(r, dc).wait_send()
                for t in range(2):
                    q_copy(t, r, dc).wait_send()
    for d in range(1, 4):
        ry_copy(d).wait_send()
        for t in range(2):
            kv_copy(t, d).wait_send()
    x_copy(0).wait_send()
    rx_copy(0).wait_send()
    for seg in range(2):
        c_copy(seg).wait_send()
        rc_copy(seg).wait_send()

    @pl.when(has_next)
    def _():
        x_copy(1).wait_send()
        x_copy(2).wait_send()

    @pl.when(has_prev)
    def _():
        for seg in (2, 3):
            c_copy(seg).wait_send()
            rc_copy(seg).wait_send()
            rx_copy(seg - 1).wait_send()


def on_device(queries, keys, values, output_gradient, span_order):
    vmem = pl.BlockSpec(memory_space=pltpu.VMEM)
    dma = pltpu.SemaphoreType.DMA
    return pl.pallas_call(
        kernel,
        out_shape=[
            jax.ShapeDtypeStruct(queries.shape, BF16),
            jax.ShapeDtypeStruct(keys.shape, BF16),
            jax.ShapeDtypeStruct(values.shape, BF16),
        ],
        in_specs=[vmem, vmem, vmem, vmem, pl.BlockSpec(memory_space=pltpu.SMEM)],
        out_specs=[vmem, vmem, vmem],
        scratch_shapes=[
            pltpu.VMEM((4, SET, COLS), BF16),
            pltpu.VMEM((4, SET, COLS), BF16),
            pltpu.VMEM((2, NKEY, HEAD), BF16),
            pltpu.VMEM((8, NKEY), F32),
            pltpu.VMEM((4, SET, 128), F32),
            pltpu.VMEM((HEAD, ROWS), BF16),
            pltpu.VMEM((HEAD, ROWS), BF16),
            pltpu.VMEM((ROWS, NKEY), F32),
            pltpu.VMEM((ROWS, NKEY), F32),
            pltpu.VMEM((ROWS, NKEY), BF16),
            pltpu.VMEM((ROWS, 128), F32),
            pltpu.VMEM((ROWS, 128), F32),
            pltpu.VMEM((ROWS, 128), F32),
            pltpu.VMEM((ROWS, HEAD), F32),
            pltpu.VMEM((32, HEAD, 128), F32),
            pltpu.VMEM((32, HEAD, 128), F32),
            pltpu.VMEM((4, SET, COLS), BF16),
            pltpu.VMEM((4, 2, 4, HEAD, 128), BF16),
            pltpu.VMEM((4, 2, 4, HEAD, 128), BF16),
            pltpu.VMEM((3, 2, 4, HEAD, 128), BF16),
            pltpu.VMEM((3, 2, 4, HEAD, 128), BF16),
            pltpu.VMEM((4, 2, HEAD, 128), BF16),
            pltpu.VMEM((4, 2, HEAD, 128), BF16),
            dma((2, 4, 2)), dma((2, 4, 2)),
            dma((2, 3)), dma((2, 3)),
            dma((3,)), dma((3,)),
            dma((4,)), dma((4,)),
            dma((5,)),
            dma((4, 2)), dma((4, 2)),
            dma((4,)), dma((4,)),
            dma((3,)), dma((3,)),
            dma((3,)), dma((3,)),
        ],
        compiler_params=pltpu.CompilerParams(
            collective_id=0, has_side_effects=True, vmem_limit_bytes=60 * 2**20
        ),
        name="attention_backward",
    )(queries, keys, values, output_gradient, span_order)


def solution(mesh):
    rows = P(("outer", "inner"), None)
    return jax.shard_map(
        on_device,
        mesh=mesh,
        in_specs=(rows, rows, rows, rows, P()),
        out_specs=(rows, rows, rows),
        check_vma=False,
    )
```

```python
import jax
import jax.numpy as jnp
from jax import lax
from jax.experimental import pallas as pl
from jax.experimental.pallas import tpu as pltpu
from jax.sharding import PartitionSpec as P

MESH = pl.DeviceIdType.MESH
F32 = jnp.float32
BF16 = jnp.bfloat16
SCALE = 128**-0.5
SCALE2 = SCALE * 1.4426950408889634
MASKED = -1.0e30
NT = (((1,), (1,)), ((), ()))

HEAD = 128
TOK = 128
NH = 3
SET = 2 * TOK
ROWS = NH * SET
COLS = NH * HEAD
SEG = 8 * TOK
NKEY = 4 * SEG
VR = 16


def kernel(
    q_ref, k_ref, v_ref, do_ref, span_ref,
    gq_ref, gk_ref, gv_ref,
    qraw, doraw, kvg, pk, pq, qt, dot, s_buf, dp_buf, e_buf, mx, ls, dd, dqa, dka, dva, dqs,
    cx, rx, xs, xr, ys, yr,
    q_ssem, q_rsem, y_ssem, y_rsem, x_ssem, x_rsem, c_ssem, c_rsem, l_sem,
    dq_ssem, dq_rsem, rc_ssem, rc_rsem, rx_ssem, rx_rsem, ry_ssem, ry_rsem,
):
    o = lax.axis_index("outer")
    i = lax.axis_index("inner")
    y, xl, c = i // 4, (i // 2) % 2, i % 2
    has_prev = o > 0
    has_next = o < 7

    def dev(oo, yy, xx, cc):
        return (oo, yy * 4 + xx * 2 + cc)

    def yrel(d):
        return lax.rem(y + d, 4)

    def remote(src, dst, ssem, rsem, device):
        return pltpu.make_async_remote_copy(
            src_ref=src, dst_ref=dst, send_sem=ssem, recv_sem=rsem, device_id=device, device_id_type=MESH
        )

    o_next, o_prev = lax.rem(o + 1, 8), lax.rem(o + 7, 8)
    core = dev(o, y, xl, 1 - c)

    barrier = pltpu.get_barrier_semaphore()
    peers = [dev(o, yrel(d), xl, cc) for d in range(1, 4) for cc in range(2)]
    peers += [core, dev(o, y, 1 - xl, c)]
    peers += [dev(oo, y, xx, c) for oo in (o_next, o_prev) for xx in range(2)]
    for p in peers:
        pl.semaphore_signal(barrier, inc=1, device_id=p, device_id_type=MESH)
    pl.semaphore_wait(barrier, len(peers))

    def rows(seg, cc, yy=0, n=4):
        return pl.ds(pl.multiple_of(seg * SEG + cc * 4 * TOK + yy * TOK, TOK), n * TOK)

    def kv_copy(t, d):
        yy = yrel(d)
        src = (k_ref, v_ref)[t].at[:, pl.ds(pl.multiple_of(yy * HEAD, HEAD), HEAD)]
        return remote(src, kvg.at[t, rows(0, c, y, 1)], y_ssem.at[t, d - 1], y_rsem.at[t, 3 - d], dev(o, yy, xl, c))

    def kv_local(t):
        src = (k_ref, v_ref)[t].at[:, pl.ds(pl.multiple_of(y * HEAD, HEAD), HEAD)]
        return pltpu.make_async_copy(src, kvg.at[t, rows(0, c, y, 1)], l_sem.at[t])

    def q_copy(t, d, dc):
        yy, cc = yrel(d), (1 - c if dc else c)
        src = (q_ref, do_ref)[t].at[:, pl.ds(pl.multiple_of((yy * 2 + cc) * COLS, 128), COLS)]
        r = lax.rem(4 - d, 4)
        dst = (qraw, doraw)[t].at[r, pl.ds(pl.multiple_of(c * TOK, TOK), TOK)]
        return remote(src, dst, q_ssem.at[t, d, dc], q_rsem.at[t, r, dc], dev(o, yy, xl, cc))

    def q_local(t):
        src = (q_ref, do_ref)[t].at[:, pl.ds(pl.multiple_of((y * 2 + c) * COLS, 128), COLS)]
        dst = (qraw, doraw)[t].at[0, pl.ds(pl.multiple_of(c * TOK, TOK), TOK)]
        return pltpu.make_async_copy(src, dst, l_sem.at[2 + t])

    def x_copy(n, d):
        yy = yrel(d)
        src = kvg.at[:, rows(0, c, yy, 1)]
        if n == 0:
            dst, device, slot = kvg.at[:, rows(1, c, yy, 1)], dev(o, y, 1 - xl, c), 0
        else:
            dst, device, slot = kvg.at[:, rows(2 + xl, c, yy, 1)], dev(o_next, y, n - 1, c), 1 + xl
        return remote(src, dst, x_ssem.at[n, d], x_rsem.at[slot, d], device)

    def x_arrival(n, d):
        dst = kvg.at[:, rows(1 + n, c, yrel(d), 1)]
        return remote(dst, dst, x_ssem.at[0, 0], x_rsem.at[n, d], core)

    def c_copy(seg):
        blk = kvg.at[:, rows(seg, c)]
        return remote(blk, blk, c_ssem.at[seg], c_rsem.at[seg], core)

    def c_arrival(seg):
        blk = kvg.at[:, rows(seg, 1 - c)]
        return remote(blk, blk, c_ssem.at[seg], c_rsem.at[seg], core)

    for t in range(2):
        kv_local(t).start()
        for d in (1, 3, 2):
            kv_copy(t, d).start()
    for t in range(2):
        q_local(t).start()
        q_copy(t, 0, 1).start()

    def send_column(d):
        x_copy(0, d).start()

        @pl.when(has_next)
        def _():
            x_copy(1, d).start()
            x_copy(2, d).start()

    for t in range(2):
        kv_local(t).wait()
    send_column(0)
    for d in (3, 1, 2):
        for dc in range(2):
            for t in range(2):
                q_copy(t, d, dc).start()

    def pk_row(blk, value):
        pk[blk] = value

    lane = lax.broadcasted_iota(jnp.int32, (8, TOK), 1)
    for xx in range(2):
        for cc in range(2):
            for yy in range(4):
                first = 2 * (yy * 4 + xx * 2 + cc)
                span = jnp.where(lane < 64, span_ref[first], span_ref[first + 1])
                blk = jnp.where(xl == xx, 0, 8) + cc * 4 + yy
                pk_row(blk, (span * 64 + lax.rem(lane, 64)).astype(F32))
    for blk in range(16, 32):
        pk_row(blk, jnp.full((8, TOK), -1.0, F32))
    sub = lax.broadcasted_iota(jnp.int32, (64, 128), 0)
    for rel in range(4):
        for cc in range(2):
            for hb in range(2):
                span = span_ref[2 * (yrel(rel) * 4 + xl * 2 + cc) + hb]
                at = (cc * 2 + hb) * 64
                pq[rel, at : at + 64, :] = (span * 64 + sub).astype(F32)

    dka[...] = jnp.zeros_like(dka)
    dva[...] = jnp.zeros_like(dva)

    for d in (3, 1, 2):
        for t in range(2):
            kv_copy(t, 4 - d).wait_recv()
        send_column(d)
    c_copy(0).start()
    c_arrival(0).wait_recv()
    for d in range(4):
        x_arrival(0, d).wait_recv()
    c_copy(1).start()
    for t in range(2):
        q_local(t).wait()
        q_copy(t, 0, 1).wait_recv()
    c_arrival(1).wait_recv()

    def take_previous():
        for n in (1, 2):
            for d in range(4):
                x_arrival(n, d).wait_recv()
            c_copy(1 + n).start()
        for n in (1, 2):
            c_arrival(1 + n).wait_recv()

    mine = pl.ds(pl.multiple_of((y * 2 + c) * COLS, 128), COLS)

    def dq_copy(r, dc):
        cc = 1 - c if dc else c
        src = dqs.at[r, pl.ds(pl.multiple_of(cc * TOK, TOK), TOK)]
        return remote(
            src,
            gq_ref.at[:, mine],
            dq_ssem.at[r, dc],
            dq_rsem.at[lax.rem(4 - r, 4), dc],
            dev(o, yrel(r), xl, cc),
        )

    def dq_arrival(r, dc):
        cc = 1 - c if dc else c
        dst = gq_ref.at[:, pl.ds(pl.multiple_of((yrel(r) * 2 + cc) * COLS, 128), COLS)]
        return remote(dst, dst, dq_ssem.at[0, 1], dq_rsem.at[r, dc], core)

    dq_local = pltpu.make_async_copy(
        dqs.at[0, pl.ds(pl.multiple_of(c * TOK, TOK), TOK)], gq_ref.at[:, mine], l_sem.at[4]
    )

    acc = (dka, dva)

    def rc_copy(seg):
        return remote(cx.at[seg], rx.at[seg], rc_ssem.at[seg], rc_rsem.at[seg], core)

    def rx_copy(n):
        if n == 0:
            return remote(xs.at[0], xr.at[0], rx_ssem.at[0], rx_rsem.at[0], dev(o, y, 1 - xl, c))
        return remote(xs.at[n], xr.at[1 + xl], rx_ssem.at[n], rx_rsem.at[1 + xl], dev(o_prev, y, n - 1, c))

    def rx_arrival(n):
        return remote(xr.at[n], xr.at[n], rx_ssem.at[0], rx_rsem.at[n], core)

    def ry_copy(d):
        yy = yrel(d)
        return remote(ys.at[yy], yr.at[y], ry_ssem.at[d - 1], ry_rsem.at[3 - d], dev(o, yy, xl, c))

    def ry_arrival(r):
        dst = yr.at[yrel(r)]
        return remote(dst, dst, ry_ssem.at[0], ry_rsem.at[r - 1], core)

    def send_core(seg):
        def step(yy, _):
            for t in range(2):
                cx[seg, t, yy] = acc[t][seg * 8 + (1 - c) * 4 + yy].astype(BF16)
            return 0

        lax.fori_loop(0, 4, step, 0)
        rc_copy(seg).start()

    def send_x(seg):
        rc_copy(seg).wait_recv()

        def step(yy, _):
            for t in range(2):
                xs[seg - 1, t, yy] = (acc[t][seg * 8 + c * 4 + yy] + rx[seg, t, yy].astype(F32)).astype(BF16)
            return 0

        lax.fori_loop(0, 4, step, 0)
        rx_copy(seg - 1).start()

    npair = jnp.where(has_prev, 2, 1)
    nl = SEG // 128

    def row_set(rel, _):
        @pl.when(rel > 0)
        def _():
            for dc in range(2):
                for t in range(2):
                    q_copy(t, 4 - rel, dc).wait_recv()

        mx[...] = jnp.full(mx.shape, MASKED, F32)

        def scores(pair, _):
            @pl.when((rel == 0) & (pair == 1))
            def _():
                take_previous()

            for half in range(2):
                b = pair * 2 + half
                keys = kvg[0, pl.ds(pl.multiple_of(b * SEG, SEG), SEG), :]
                for h in range(NH):
                    r = slice(h * SET, h * SET + SET)
                    s = lax.dot_general(
                        qraw[rel, :, h * HEAD : h * HEAD + HEAD], keys, NT, preferred_element_type=F32
                    )
                    m = mx[r, :]
                    for j in range(nl):
                        at = slice(j * 128, j * 128 + 128)
                        sj = jnp.where(pk[b * nl + j, 0:1, :] <= pq[rel], s[:, at], MASKED)
                        m = jnp.maximum(m, sj)
                        s_buf[b, r, at] = sj
                    mx[r, :] = m
            return 0

        lax.fori_loop(0, npair, scores, 0)
        for h in range(NH):
            r = slice(h * SET, h * SET + SET)
            mx[r, :] = jnp.broadcast_to(jnp.max(mx[r, :], axis=1, keepdims=True) * SCALE2, (SET, 128))
        ls[...] = jnp.zeros_like(ls)
        dd[...] = jnp.zeros_like(dd)

        def weights(pair, _):
            for half in range(2):
                b = pair * 2 + half
                vals = kvg[1, pl.ds(pl.multiple_of(b * SEG, SEG), SEG), :]
                for h in range(NH):
                    dp = lax.dot_general(
                        doraw[rel, :, h * HEAD : h * HEAD + HEAD], vals, NT, preferred_element_type=F32
                    )
                    for g0 in range(0, SET, VR):
                        g = slice(h * SET + g0, h * SET + g0 + VR)
                        m, l, d = mx[g, :], ls[g, :], dd[g, :]
                        for j in range(nl):
                            at = slice(j * 128, j * 128 + 128)
                            e = jnp.exp2(s_buf[b, g, at] * SCALE2 - m)
                            dpj = dp[g0 : g0 + VR, at]
                            l = l + e
                            d = d + e * dpj
                            e_buf[b, g, at] = e.astype(BF16)
                            dp_buf[b, g, at] = dpj
                        ls[g, :] = l
                        dd[g, :] = d
            return 0

        lax.fori_loop(0, npair, weights, 0)
        for h in range(NH):
            r = slice(h * SET, h * SET + SET)
            rinv = 1.0 / jnp.sum(ls[r, :], axis=1, keepdims=True)
            delta = jnp.sum(dd[r, :], axis=1, keepdims=True) * rinv
            ls[r, :] = jnp.broadcast_to(rinv, (SET, 128))
            dd[r, :] = jnp.broadcast_to(delta, (SET, 128))
            hc = slice(h * HEAD, h * HEAD + HEAD)
            qt[:, r] = (qraw[rel, :, hc].astype(F32) * rinv).astype(BF16).T
            dot[:, r] = (doraw[rel, :, hc].astype(F32) * rinv).astype(BF16).T
        dqa[...] = jnp.zeros_like(dqa)

        def grads(step, _):
            pair = npair - 1 - step
            for half in range(2):
                b = pair * 2 + half
                keys = kvg[0, pl.ds(pl.multiple_of(b * SEG, SEG), SEG), :]
                dv = jnp.dot(dot[...], e_buf[b], preferred_element_type=F32)
                dk = None
                for h in range(NH):
                    r = slice(h * SET, h * SET + SET)
                    parts = []
                    for g0 in range(0, SET, VR):
                        g = slice(h * SET + g0, h * SET + g0 + VR)
                        d = dd[g, :]
                        part = []
                        for j in range(nl):
                            at = slice(j * 128, j * 128 + 128)
                            part.append((e_buf[b, g, at].astype(F32) * (dp_buf[b, g, at] - d)).astype(BF16))
                        parts.append(jnp.concatenate(part, axis=1))
                    ds = jnp.concatenate(parts, axis=0)
                    dqa[r, :] += jnp.dot(ds, keys, preferred_element_type=F32)
                    part = jnp.dot(qt[:, r], ds, preferred_element_type=F32)
                    dk = part if dk is None else dk + part
                for j in range(nl):
                    blk = b * nl + j
                    dva[blk] += dv[:, j * 128 : j * 128 + 128]
                    dka[blk] += dk[:, j * 128 : j * 128 + 128]

            @pl.when((rel == 3) & (pair == 1))
            def _():
                send_core(2)
                send_core(3)

            return 0

        lax.fori_loop(0, npair, grads, 0)
        for h in range(NH):
            r = slice(h * SET, h * SET + SET)
            dqs[rel, :, h * HEAD : h * HEAD + HEAD] = (dqa[r, :] * (ls[r, :] * SCALE)).astype(BF16)

        @pl.when(rel > 0)
        def _():
            dq_copy(rel, 0).start()

        @pl.when(rel == 0)
        def _():
            dq_local.start()

        dq_copy(rel, 1).start()
        return 0

    lax.fori_loop(0, 4, row_set, 0)

    send_core(1)
    send_core(0)

    @pl.when(has_prev)
    def _():
        send_x(2)
        send_x(3)

    send_x(1)
    rc_copy(0).wait_recv()

    def own(yy, _):
        for t in range(2):
            blk = c * 4 + yy
            acc[t][blk] = acc[t][blk] + rx[0, t, yy].astype(F32)
        return 0

    lax.fori_loop(0, 4, own, 0)

    def take(n):
        rx_arrival(n).wait_recv()

        def step(yy, _):
            for t in range(2):
                blk = c * 4 + yy
                acc[t][blk] = acc[t][blk] + xr[n, t, yy].astype(F32)
            return 0

        lax.fori_loop(0, 4, step, 0)

    take(0)

    @pl.when(has_next)
    def _():
        take(1)
        take(2)

    def final(yy, _):
        blk = c * 4 + yy
        ys[yy, 0] = (acc[0][blk] * SCALE).astype(BF16)
        ys[yy, 1] = acc[1][blk].astype(BF16)
        return 0

    lax.fori_loop(0, 4, final, 0)
    for d in range(1, 4):
        ry_copy(d).start()
    outs = (gk_ref, gv_ref)
    at_me = pl.ds(pl.multiple_of(y * HEAD, HEAD), HEAD)
    for t in range(2):
        outs[t][:, at_me] = ys[y, t].T
    for r in range(1, 4):
        ry_arrival(r).wait_recv()
        at = pl.ds(pl.multiple_of(yrel(r) * HEAD, HEAD), HEAD)
        for t in range(2):
            outs[t][:, at] = yr[yrel(r), t].T

    dq_local.wait()
    for r in range(4):
        for dc in range(2):
            if r or dc:
                dq_arrival(r, dc).wait_recv()
                dq_copy(r, dc).wait_send()
                for t in range(2):
                    q_copy(t, r, dc).wait_send()
    for d in range(1, 4):
        ry_copy(d).wait_send()
        for t in range(2):
            kv_copy(t, d).wait_send()
    for d in range(4):
        x_copy(0, d).wait_send()
    rx_copy(0).wait_send()
    for seg in range(2):
        c_copy(seg).wait_send()
        rc_copy(seg).wait_send()

    @pl.when(has_next)
    def _():
        for d in range(4):
            x_copy(1, d).wait_send()
            x_copy(2, d).wait_send()

    @pl.when(has_prev)
    def _():
        for seg in (2, 3):
            c_copy(seg).wait_send()
            rc_copy(seg).wait_send()
            rx_copy(seg - 1).wait_send()


def on_device(queries, keys, values, output_gradient, span_order):
    vmem = pl.BlockSpec(memory_space=pltpu.VMEM)
    dma = pltpu.SemaphoreType.DMA
    return pl.pallas_call(
        kernel,
        out_shape=[
            jax.ShapeDtypeStruct(queries.shape, BF16),
            jax.ShapeDtypeStruct(keys.shape, BF16),
            jax.ShapeDtypeStruct(values.shape, BF16),
        ],
        in_specs=[vmem, vmem, vmem, vmem, pl.BlockSpec(memory_space=pltpu.SMEM)],
        out_specs=[vmem, vmem, vmem],
        scratch_shapes=[
            pltpu.VMEM((4, SET, COLS), BF16),
            pltpu.VMEM((4, SET, COLS), BF16),
            pltpu.VMEM((2, NKEY, HEAD), BF16),
            pltpu.VMEM((32, 8, TOK), F32),
            pltpu.VMEM((4, SET, 128), F32),
            pltpu.VMEM((HEAD, ROWS), BF16),
            pltpu.VMEM((HEAD, ROWS), BF16),
            pltpu.VMEM((4, ROWS, SEG), F32),
            pltpu.VMEM((4, ROWS, SEG), F32),
            pltpu.VMEM((4, ROWS, SEG), BF16),
            pltpu.VMEM((ROWS, 128), F32),
            pltpu.VMEM((ROWS, 128), F32),
            pltpu.VMEM((ROWS, 128), F32),
            pltpu.VMEM((ROWS, HEAD), F32),
            pltpu.VMEM((32, HEAD, 128), F32),
            pltpu.VMEM((32, HEAD, 128), F32),
            pltpu.VMEM((4, SET, COLS), BF16),
            pltpu.VMEM((4, 2, 4, HEAD, 128), BF16),
            pltpu.VMEM((4, 2, 4, HEAD, 128), BF16),
            pltpu.VMEM((3, 2, 4, HEAD, 128), BF16),
            pltpu.VMEM((3, 2, 4, HEAD, 128), BF16),
            pltpu.VMEM((4, 2, HEAD, 128), BF16),
            pltpu.VMEM((4, 2, HEAD, 128), BF16),
            dma((2, 4, 2)), dma((2, 4, 2)),
            dma((2, 3)), dma((2, 3)),
            dma((3, 4)), dma((3, 4)),
            dma((4,)), dma((4,)),
            dma((5,)),
            dma((4, 2)), dma((4, 2)),
            dma((4,)), dma((4,)),
            dma((3,)), dma((3,)),
            dma((3,)), dma((3,)),
        ],
        compiler_params=pltpu.CompilerParams(
            collective_id=0, has_side_effects=True, vmem_limit_bytes=60 * 2**20
        ),
        name="attention_backward",
    )(queries, keys, values, output_gradient, span_order)


def solution(mesh):
    rows = P(("outer", "inner"), None)
    return jax.shard_map(
        on_device,
        mesh=mesh,
        in_specs=(rows, rows, rows, rows, P()),
        out_specs=(rows, rows, rows),
        check_vma=False,
    )
```

```python
import jax
import jax.numpy as jnp
from jax import lax
from jax.experimental import pallas as pl
from jax.experimental.pallas import tpu as pltpu
from jax.sharding import PartitionSpec as P

MESH = pl.DeviceIdType.MESH
F32 = jnp.float32
BF16 = jnp.bfloat16
SCALE = 128**-0.5
SCALE2 = SCALE * 1.4426950408889634
MASKED = -1.0e30
NT = (((1,), (1,)), ((), ()))

HEAD = 128
TOK = 128
NH = 3
SET = 2 * TOK
ROWS = NH * SET
COLS = NH * HEAD
SEG = 8 * TOK
NKEY = 4 * SEG
VR = 16


def kernel(
    q_ref, k_ref, v_ref, do_ref, span_ref,
    gq_ref, gk_ref, gv_ref,
    qraw, doraw, kvg, pk, pq, qt, dot, s_buf, e_buf, mx, wgt, st_l, st_d, dqp, dka, dva, dqs,
    cx, rx, xs, xr, ys, yr,
    q_ssem, q_rsem, y_ssem, y_rsem, x_ssem, x_rsem, c_ssem, c_rsem, l_sem,
    dq_ssem, dq_rsem, rc_ssem, rc_rsem, rx_ssem, rx_rsem, ry_ssem, ry_rsem,
):
    o = lax.axis_index("outer")
    i = lax.axis_index("inner")
    y, xl, c = i // 4, (i // 2) % 2, i % 2
    has_prev = o > 0
    has_next = o < 7

    def dev(oo, yy, xx, cc):
        return (oo, yy * 4 + xx * 2 + cc)

    def yrel(d):
        return lax.rem(y + d, 4)

    def remote(src, dst, ssem, rsem, device):
        return pltpu.make_async_remote_copy(
            src_ref=src, dst_ref=dst, send_sem=ssem, recv_sem=rsem, device_id=device, device_id_type=MESH
        )

    o_next, o_prev = lax.rem(o + 1, 8), lax.rem(o + 7, 8)
    core = dev(o, y, xl, 1 - c)

    barrier = pltpu.get_barrier_semaphore()
    peers = [dev(o, yrel(d), xl, cc) for d in range(1, 4) for cc in range(2)]
    peers += [core, dev(o, y, 1 - xl, c)]
    peers += [dev(oo, y, xx, c) for oo in (o_next, o_prev) for xx in range(2)]
    for p in peers:
        pl.semaphore_signal(barrier, inc=1, device_id=p, device_id_type=MESH)
    pl.semaphore_wait(barrier, len(peers))

    def rows(seg, cc, yy=0, n=4):
        return pl.ds(pl.multiple_of(seg * SEG + cc * 4 * TOK + yy * TOK, TOK), n * TOK)

    def kv_copy(t, d):
        yy = yrel(d)
        src = (k_ref, v_ref)[t].at[:, pl.ds(pl.multiple_of(yy * HEAD, HEAD), HEAD)]
        return remote(src, kvg.at[t, rows(0, c, y, 1)], y_ssem.at[t, d - 1], y_rsem.at[t, 3 - d], dev(o, yy, xl, c))

    def kv_local(t):
        src = (k_ref, v_ref)[t].at[:, pl.ds(pl.multiple_of(y * HEAD, HEAD), HEAD)]
        return pltpu.make_async_copy(src, kvg.at[t, rows(0, c, y, 1)], l_sem.at[t])

    def q_copy(t, d, dc):
        yy, cc = yrel(d), (1 - c if dc else c)
        src = (q_ref, do_ref)[t].at[:, pl.ds(pl.multiple_of((yy * 2 + cc) * COLS, 128), COLS)]
        r = lax.rem(4 - d, 4)
        dst = (qraw, doraw)[t].at[r, pl.ds(pl.multiple_of(c * TOK, TOK), TOK)]
        return remote(src, dst, q_ssem.at[t, d, dc], q_rsem.at[t, r, dc], dev(o, yy, xl, cc))

    def q_local(t):
        src = (q_ref, do_ref)[t].at[:, pl.ds(pl.multiple_of((y * 2 + c) * COLS, 128), COLS)]
        dst = (qraw, doraw)[t].at[0, pl.ds(pl.multiple_of(c * TOK, TOK), TOK)]
        return pltpu.make_async_copy(src, dst, l_sem.at[2 + t])

    def x_copy(n, d):
        yy = yrel(d)
        src = kvg.at[:, rows(0, c, yy, 1)]
        if n == 0:
            dst, device, slot = kvg.at[:, rows(1, c, yy, 1)], dev(o, y, 1 - xl, c), 0
        else:
            dst, device, slot = kvg.at[:, rows(2 + xl, c, yy, 1)], dev(o_next, y, n - 1, c), 1 + xl
        return remote(src, dst, x_ssem.at[n, d], x_rsem.at[slot, d], device)

    def x_arrival(n, d):
        dst = kvg.at[:, rows(1 + n, c, yrel(d), 1)]
        return remote(dst, dst, x_ssem.at[0, 0], x_rsem.at[n, d], core)

    def c_copy(seg):
        blk = kvg.at[:, rows(seg, c)]
        return remote(blk, blk, c_ssem.at[seg], c_rsem.at[seg], core)

    def c_arrival(seg):
        blk = kvg.at[:, rows(seg, 1 - c)]
        return remote(blk, blk, c_ssem.at[seg], c_rsem.at[seg], core)

    for t in range(2):
        kv_local(t).start()
        for d in (1, 3, 2):
            kv_copy(t, d).start()
    for t in range(2):
        q_local(t).start()
        q_copy(t, 0, 1).start()

    def send_next(d):
        @pl.when(has_next)
        def _():
            x_copy(1, d).start()
            x_copy(2, d).start()

    for t in range(2):
        kv_local(t).wait()
    x_copy(0, 0).start()
    send_next(0)
    def pk_row(blk, value):
        pk[blk] = value

    lane = lax.broadcasted_iota(jnp.int32, (8, TOK), 1)
    for xx in range(2):
        for cc in range(2):
            for yy in range(4):
                first = 2 * (yy * 4 + xx * 2 + cc)
                span = jnp.where(lane < 64, span_ref[first], span_ref[first + 1])
                blk = jnp.where(xl == xx, 0, 8) + cc * 4 + yy
                pk_row(blk, (span * 64 + lax.rem(lane, 64)).astype(F32))
    for blk in range(16, 32):
        pk_row(blk, jnp.full((8, TOK), -1.0, F32))
    sub = lax.broadcasted_iota(jnp.int32, (64, 128), 0)
    for rel in range(4):
        for cc in range(2):
            for hb in range(2):
                span = span_ref[2 * (yrel(rel) * 4 + xl * 2 + cc) + hb]
                at = (cc * 2 + hb) * 64
                pq[rel, at : at + 64, :] = (span * 64 + sub).astype(F32)

    dka[...] = jnp.zeros_like(dka)
    dva[...] = jnp.zeros_like(dva)

    for d in (3, 1, 2):
        for t in range(2):
            kv_copy(t, 4 - d).wait_recv()
        x_copy(0, d).start()
    for d in (3, 1):
        for dc in range(2):
            for t in range(2):
                q_copy(t, d, dc).start()
    for d in (3, 1, 2):
        send_next(d)
    c_copy(0).start()
    c_arrival(0).wait_recv()
    for d in range(4):
        x_arrival(0, d).wait_recv()
    c_copy(1).start()
    for t in range(2):
        q_local(t).wait()
        q_copy(t, 0, 1).wait_recv()
    c_arrival(1).wait_recv()

    def take_previous():
        for n in (1, 2):
            for d in range(4):
                x_arrival(n, d).wait_recv()
            c_copy(1 + n).start()
        for n in (1, 2):
            c_arrival(1 + n).wait_recv()

    mine = pl.ds(pl.multiple_of((y * 2 + c) * COLS, 128), COLS)

    def dq_copy(r, dc):
        cc = 1 - c if dc else c
        src = dqs.at[r, pl.ds(pl.multiple_of(cc * TOK, TOK), TOK)]
        return remote(
            src,
            gq_ref.at[:, mine],
            dq_ssem.at[r, dc],
            dq_rsem.at[lax.rem(4 - r, 4), dc],
            dev(o, yrel(r), xl, cc),
        )

    def dq_arrival(r, dc):
        cc = 1 - c if dc else c
        dst = gq_ref.at[:, pl.ds(pl.multiple_of((yrel(r) * 2 + cc) * COLS, 128), COLS)]
        return remote(dst, dst, dq_ssem.at[0, 1], dq_rsem.at[r, dc], core)

    dq_local = pltpu.make_async_copy(
        dqs.at[0, pl.ds(pl.multiple_of(c * TOK, TOK), TOK)], gq_ref.at[:, mine], l_sem.at[4]
    )

    acc = (dka, dva)

    def rc_copy(seg):
        return remote(cx.at[seg], rx.at[seg], rc_ssem.at[seg], rc_rsem.at[seg], core)

    def rx_copy(n):
        if n == 0:
            return remote(xs.at[0], xr.at[0], rx_ssem.at[0], rx_rsem.at[0], dev(o, y, 1 - xl, c))
        return remote(xs.at[n], xr.at[1 + xl], rx_ssem.at[n], rx_rsem.at[1 + xl], dev(o_prev, y, n - 1, c))

    def rx_arrival(n):
        return remote(xr.at[n], xr.at[n], rx_ssem.at[0], rx_rsem.at[n], core)

    def ry_copy(d):
        yy = yrel(d)
        return remote(ys.at[yy], yr.at[y], ry_ssem.at[d - 1], ry_rsem.at[3 - d], dev(o, yy, xl, c))

    def ry_arrival(r):
        dst = yr.at[yrel(r)]
        return remote(dst, dst, ry_ssem.at[0], ry_rsem.at[r - 1], core)

    def send_core(seg):
        def step(yy, _):
            for t in range(2):
                cx[seg, t, yy] = acc[t][seg * 8 + (1 - c) * 4 + yy].astype(BF16)
            return 0

        lax.fori_loop(0, 4, step, 0)
        rc_copy(seg).start()

    def send_x(seg):
        rc_copy(seg).wait_recv()

        def step(yy, _):
            for t in range(2):
                xs[seg - 1, t, yy] = (acc[t][seg * 8 + c * 4 + yy] + rx[seg, t, yy].astype(F32)).astype(BF16)
            return 0

        lax.fori_loop(0, 4, step, 0)
        rx_copy(seg - 1).start()

    nl = SEG // 128
    hrows = [slice(h * SET, h * SET + SET) for h in range(NH)]
    hcols = [slice(h * HEAD, h * HEAD + HEAD) for h in range(NH)]

    def lanes(j):
        return slice(j * 128, j * 128 + 128)

    def keys_of(t, seg):
        return kvg[t, seg * SEG : seg * SEG + SEG, :]

    def scores(rel, first, masked):
        for half in range(2):
            keys = keys_of(0, first + half)
            for h in range(NH):
                r = hrows[h]
                s = lax.dot_general(qraw[rel, :, hcols[h]], keys, NT, preferred_element_type=F32)
                m = mx[r, :]
                for j in range(nl):
                    sj = s[:, lanes(j)] * SCALE2
                    if masked:
                        sj = jnp.where(pk[(first + half) * nl + j, 0:1, :] <= pq[rel], sj, MASKED)
                    m = jnp.maximum(m, sj)
                    s_buf[half, r, lanes(j)] = sj
                mx[r, :] = m

    def weights(rel, first):
        for half in range(2):
            vals = keys_of(1, first + half)
            for h in range(NH):
                dp = lax.dot_general(doraw[rel, :, hcols[h]], vals, NT, preferred_element_type=F32)
                for g0 in range(0, SET, VR):
                    g = slice(h * SET + g0, h * SET + g0 + VR)
                    m, l, d = mx[g, :], st_l[rel, g, :], st_d[rel, g, :]
                    for j in range(nl):
                        e = jnp.exp2(s_buf[half, g, lanes(j)] - m)
                        dpj = dp[g0 : g0 + VR, lanes(j)]
                        l = l + e
                        d = d + e * dpj
                        e_buf[first + half, rel, g, lanes(j)] = e.astype(BF16)
                    st_l[rel, g, :] = l
                    st_d[rel, g, :] = d

    def scaled_t(x, w):
        return (x.astype(F32) * w).astype(BF16).T

    def own_keys(rel):
        @pl.when(rel > 0)
        def _():
            for dc in range(2):
                for t in range(2):
                    q_copy(t, 4 - rel, dc).wait_recv()

        mx[...] = jnp.full(mx.shape, MASKED, F32)
        st_l[rel] = jnp.zeros((ROWS, 128), F32)
        st_d[rel] = jnp.zeros((ROWS, 128), F32)
        dqp[rel] = jnp.zeros((ROWS, HEAD), F32)
        scores(rel, 0, True)
        for r in hrows:
            m = jnp.broadcast_to(jnp.max(mx[r, :], axis=1, keepdims=True), (SET, 128))
            mx[r, :] = m
            wgt[0, rel, r, :] = m
        weights(rel, 0)

    def previous_keys(rel):
        @pl.when(has_prev)
        def _():
            mx[...] = jnp.full(mx.shape, MASKED, F32)
            scores(rel, 2, False)
            for r in hrows:
                top = jnp.max(mx[r, :], axis=1, keepdims=True)
                before = wgt[0, rel, r, :]
                m = jnp.maximum(before, top)
                shrink = jnp.exp2(before - m)
                mx[r, :] = m
                wgt[0, rel, r, :] = shrink
                st_l[rel, r, :] = st_l[rel, r, :] * shrink
                st_d[rel, r, :] = st_d[rel, r, :] * shrink
            weights(rel, 2)

        @pl.when(jnp.logical_not(has_prev))
        def _():
            wgt[0, rel] = jnp.ones((ROWS, 128), F32)

        for h in range(NH):
            r = hrows[h]
            rinv = 1.0 / jnp.sum(st_l[rel, r, :], axis=1, keepdims=True)
            delta = jnp.sum(st_d[rel, r, :], axis=1, keepdims=True) * rinv
            st_d[rel, r, :] = jnp.broadcast_to(delta, (SET, 128))
            factors = (wgt[0, rel, r, :] * rinv, jnp.broadcast_to(rinv, (SET, 128)))
            for g in range(2):
                wgt[g, rel, r, :] = factors[g]
                qt[g, rel, :, r] = scaled_t(qraw[rel, :, hcols[h]], factors[g])
                dot[g, rel, :, r] = scaled_t(doraw[rel, :, hcols[h]], factors[g])

    def forward(step, _):
        t = jnp.where(step >= 3, step - 3, step)
        rel = jnp.where(step >= 6, 2, jnp.where(t == 2, 3, t))
        own = (step < 3) | (step == 6)

        @pl.when(step == 1)
        def _():
            for dc in range(2):
                for t in range(2):
                    q_copy(t, 2, dc).start()

        @pl.when((step == 3) & has_prev)
        def _():
            take_previous()

        @pl.when(own)
        def _():
            own_keys(rel)

        @pl.when(jnp.logical_not(own))
        def _():
            previous_keys(rel)

        return 0

    lax.fori_loop(0, 8, forward, 0)

    def gradients(it, _):
        order = it // 4
        seg = jnp.where(order < 2, order + 2, 3 - order)
        rel = lax.rem(it + 1, 4)
        grp = jnp.where(order < 2, 1, 0)

        for at, event, n in ((4, send_core, 2), (6, send_x, 2), (8, send_core, 3), (10, send_x, 3)):

            @pl.when((it == at) & has_prev)
            def _(event=event, n=n):
                event(n)

        @pl.when(it == 12)
        def _():
            send_core(1)

        @pl.when(it == 14)
        def _():
            send_x(1)

        at = pl.ds(pl.multiple_of(seg * SEG, SEG), SEG)
        keys, vals = kvg[0, at, :], kvg[1, at, :]
        dv = jnp.dot(dot[grp, rel], e_buf[seg, rel], preferred_element_type=F32)
        dk = None
        for h in range(NH):
            r = hrows[h]
            dp = lax.dot_general(doraw[rel, :, hcols[h]], vals, NT, preferred_element_type=F32)
            parts = []
            for g0 in range(0, SET, VR):
                g = slice(h * SET + g0, h * SET + g0 + VR)
                d = st_d[rel, g, :]
                part = []
                for j in range(nl):
                    e = e_buf[seg, rel, g, lanes(j)].astype(F32)
                    part.append((e * (dp[g0 : g0 + VR, lanes(j)] - d)).astype(BF16))
                parts.append(jnp.concatenate(part, axis=1))
            ds = jnp.concatenate(parts, axis=0)
            dqp[rel, r, :] += jnp.dot(ds, keys, preferred_element_type=F32) * (wgt[grp, rel, r, :] * SCALE)
            part = jnp.dot(qt[grp, rel, :, r], ds, preferred_element_type=F32)
            dk = part if dk is None else dk + part
        for j in range(nl):
            dva[seg * nl + j] += dv[:, lanes(j)]
            dka[seg * nl + j] += dk[:, lanes(j)]

        @pl.when(seg == 0)
        def _():
            for h in range(NH):
                dqs[rel, :, hcols[h]] = dqp[rel, hrows[h], :].astype(BF16)

            @pl.when(rel > 0)
            def _():
                dq_copy(rel, 0).start()

            @pl.when(rel == 0)
            def _():
                dq_local.start()

            dq_copy(rel, 1).start()

        return 0

    lax.fori_loop(jnp.where(has_prev, 0, 8), 16, gradients, 0)
    send_core(0)
    rc_copy(0).wait_recv()

    def own(yy, _):
        for t in range(2):
            blk = c * 4 + yy
            acc[t][blk] = acc[t][blk] + rx[0, t, yy].astype(F32)
        return 0

    lax.fori_loop(0, 4, own, 0)

    def take(n):
        rx_arrival(n).wait_recv()

        def step(yy, _):
            for t in range(2):
                blk = c * 4 + yy
                acc[t][blk] = acc[t][blk] + xr[n, t, yy].astype(F32)
            return 0

        lax.fori_loop(0, 4, step, 0)

    take(0)

    @pl.when(has_next)
    def _():
        take(1)
        take(2)

    def final(yy, _):
        blk = c * 4 + yy
        ys[yy, 0] = (acc[0][blk] * SCALE).astype(BF16)
        ys[yy, 1] = acc[1][blk].astype(BF16)
        return 0

    lax.fori_loop(0, 4, final, 0)
    for d in range(1, 4):
        ry_copy(d).start()
    outs = (gk_ref, gv_ref)
    at_me = pl.ds(pl.multiple_of(y * HEAD, HEAD), HEAD)
    for t in range(2):
        outs[t][:, at_me] = ys[y, t].T
    for r in range(1, 4):
        ry_arrival(r).wait_recv()
        at = pl.ds(pl.multiple_of(yrel(r) * HEAD, HEAD), HEAD)
        for t in range(2):
            outs[t][:, at] = yr[yrel(r), t].T

    dq_local.wait()
    for r in range(4):
        for dc in range(2):
            if r or dc:
                dq_arrival(r, dc).wait_recv()
                dq_copy(r, dc).wait_send()
                for t in range(2):
                    q_copy(t, r, dc).wait_send()
    for d in range(1, 4):
        ry_copy(d).wait_send()
        for t in range(2):
            kv_copy(t, d).wait_send()
    for d in range(4):
        x_copy(0, d).wait_send()
    rx_copy(0).wait_send()
    for seg in range(2):
        c_copy(seg).wait_send()
        rc_copy(seg).wait_send()

    @pl.when(has_next)
    def _():
        for d in range(4):
            x_copy(1, d).wait_send()
            x_copy(2, d).wait_send()

    @pl.when(has_prev)
    def _():
        for seg in (2, 3):
            c_copy(seg).wait_send()
            rc_copy(seg).wait_send()
            rx_copy(seg - 1).wait_send()


def on_device(queries, keys, values, output_gradient, span_order):
    vmem = pl.BlockSpec(memory_space=pltpu.VMEM)
    hbm = pl.BlockSpec(memory_space=pl.ANY)
    dma = pltpu.SemaphoreType.DMA
    return pl.pallas_call(
        kernel,
        out_shape=[
            jax.ShapeDtypeStruct(queries.shape, BF16),
            jax.ShapeDtypeStruct(keys.shape, BF16),
            jax.ShapeDtypeStruct(values.shape, BF16),
        ],
        in_specs=[hbm, vmem, vmem, hbm, pl.BlockSpec(memory_space=pltpu.SMEM)],
        out_specs=[hbm, vmem, vmem],
        scratch_shapes=[
            pltpu.VMEM((4, SET, COLS), BF16),
            pltpu.VMEM((4, SET, COLS), BF16),
            pltpu.VMEM((2, NKEY, HEAD), BF16),
            pltpu.VMEM((32, 8, TOK), F32),
            pltpu.VMEM((4, SET, 128), F32),
            pltpu.VMEM((2, 4, HEAD, ROWS), BF16),
            pltpu.VMEM((2, 4, HEAD, ROWS), BF16),
            pltpu.VMEM((2, ROWS, SEG), F32),
            pltpu.VMEM((4, 4, ROWS, SEG), BF16),
            pltpu.VMEM((ROWS, 128), F32),
            pltpu.VMEM((2, 4, ROWS, 128), F32),
            pltpu.VMEM((4, ROWS, 128), F32),
            pltpu.VMEM((4, ROWS, 128), F32),
            pltpu.VMEM((4, ROWS, HEAD), F32),
            pltpu.VMEM((32, HEAD, 128), F32),
            pltpu.VMEM((32, HEAD, 128), F32),
            pltpu.VMEM((4, SET, COLS), BF16),
            pltpu.VMEM((4, 2, 4, HEAD, 128), BF16),
            pltpu.VMEM((4, 2, 4, HEAD, 128), BF16),
            pltpu.VMEM((3, 2, 4, HEAD, 128), BF16),
            pltpu.VMEM((3, 2, 4, HEAD, 128), BF16),
            pltpu.VMEM((4, 2, HEAD, 128), BF16),
            pltpu.VMEM((4, 2, HEAD, 128), BF16),
            dma((2, 4, 2)), dma((2, 4, 2)),
            dma((2, 3)), dma((2, 3)),
            dma((3, 4)), dma((3, 4)),
            dma((4,)), dma((4,)),
            dma((5,)),
            dma((4, 2)), dma((4, 2)),
            dma((4,)), dma((4,)),
            dma((3,)), dma((3,)),
            dma((3,)), dma((3,)),
        ],
        compiler_params=pltpu.CompilerParams(
            collective_id=0, has_side_effects=True, vmem_limit_bytes=62 * 2**20
        ),
        name="attention_backward",
    )(queries, keys, values, output_gradient, span_order)


def solution(mesh):
    rows = P(("outer", "inner"), None)
    return jax.shard_map(
        on_device,
        mesh=mesh,
        in_specs=(rows, rows, rows, rows, P()),
        out_specs=(rows, rows, rows),
        check_vma=False,
    )
```

```python
import jax
import jax.numpy as jnp
from jax import lax
from jax.experimental import pallas as pl
from jax.experimental.pallas import tpu as pltpu
from jax.sharding import PartitionSpec as P

MESH = pl.DeviceIdType.MESH
F32 = jnp.float32
BF16 = jnp.bfloat16
SCALE = 128**-0.5
SCALE2 = SCALE * 1.4426950408889634
MASKED = -1.0e30
NT = (((1,), (1,)), ((), ()))

HEAD = 128
TOK = 128
NH = 3
SET = 2 * TOK
ROWS = NH * SET
COLS = NH * HEAD
SEG = 8 * TOK
NKEY = 4 * SEG
VR = 16


def kernel(
    q_ref, k_ref, v_ref, do_ref, span_ref,
    gq_ref, gk_ref, gv_ref,
    qraw, doraw, kvg, pk, pq, qt, dot, s_buf, e_buf, mx, wgt, st_l, st_d, dqp, dka, dva, dqs,
    cx, rx, xs, xr, ys, yr,
    q_ssem, q_rsem, y_ssem, y_rsem, x_ssem, x_rsem, c_ssem, c_rsem, l_sem,
    dq_ssem, dq_rsem, rc_ssem, rc_rsem, rx_ssem, rx_rsem, ry_ssem, ry_rsem,
):
    o = lax.axis_index("outer")
    i = lax.axis_index("inner")
    y, xl, c = i // 4, (i // 2) % 2, i % 2
    has_prev = o > 0
    has_next = o < 7

    def dev(oo, yy, xx, cc):
        return (oo, yy * 4 + xx * 2 + cc)

    def yrel(d):
        return lax.rem(y + d, 4)

    def remote(src, dst, ssem, rsem, device):
        return pltpu.make_async_remote_copy(
            src_ref=src, dst_ref=dst, send_sem=ssem, recv_sem=rsem, device_id=device, device_id_type=MESH
        )

    o_next, o_prev = lax.rem(o + 1, 8), lax.rem(o + 7, 8)
    core = dev(o, y, xl, 1 - c)

    barrier = pltpu.get_barrier_semaphore()
    peers = [dev(o, yrel(d), xl, cc) for d in range(1, 4) for cc in range(2)]
    peers += [core, dev(o, y, 1 - xl, c)]
    peers += [dev(oo, y, xx, c) for oo in (o_next, o_prev) for xx in range(2)]
    for p in peers:
        pl.semaphore_signal(barrier, inc=1, device_id=p, device_id_type=MESH)
    pl.semaphore_wait(barrier, len(peers))

    def rows(seg, cc, yy=0, n=4):
        return pl.ds(pl.multiple_of(seg * SEG + cc * 4 * TOK + yy * TOK, TOK), n * TOK)

    def kv_copy(t, d):
        yy = yrel(d)
        src = (k_ref, v_ref)[t].at[:, pl.ds(pl.multiple_of(yy * HEAD, HEAD), HEAD)]
        return remote(src, kvg.at[t, rows(0, c, y, 1)], y_ssem.at[t, d - 1], y_rsem.at[t, 3 - d], dev(o, yy, xl, c))

    def kv_local(t):
        src = (k_ref, v_ref)[t].at[:, pl.ds(pl.multiple_of(y * HEAD, HEAD), HEAD)]
        return pltpu.make_async_copy(src, kvg.at[t, rows(0, c, y, 1)], l_sem.at[t])

    def q_copy(t, d, dc):
        yy, cc = yrel(d), (1 - c if dc else c)
        src = (q_ref, do_ref)[t].at[:, pl.ds(pl.multiple_of((yy * 2 + cc) * COLS, 128), COLS)]
        r = lax.rem(4 - d, 4)
        dst = (qraw, doraw)[t].at[r, pl.ds(pl.multiple_of(c * TOK, TOK), TOK)]
        return remote(src, dst, q_ssem.at[t, d, dc], q_rsem.at[t, r, dc], dev(o, yy, xl, cc))

    def q_local(t):
        src = (q_ref, do_ref)[t].at[:, pl.ds(pl.multiple_of((y * 2 + c) * COLS, 128), COLS)]
        dst = (qraw, doraw)[t].at[0, pl.ds(pl.multiple_of(c * TOK, TOK), TOK)]
        return pltpu.make_async_copy(src, dst, l_sem.at[2 + t])

    def x_copy(n, d):
        yy = yrel(d)
        src = kvg.at[:, rows(0, c, yy, 1)]
        if n == 0:
            dst, device, slot = kvg.at[:, rows(1, c, yy, 1)], dev(o, y, 1 - xl, c), 0
        else:
            dst, device, slot = kvg.at[:, rows(2 + xl, c, yy, 1)], dev(o_next, y, n - 1, c), 1 + xl
        return remote(src, dst, x_ssem.at[n, d], x_rsem.at[slot, d], device)

    def x_arrival(n, d):
        dst = kvg.at[:, rows(1 + n, c, yrel(d), 1)]
        return remote(dst, dst, x_ssem.at[0, 0], x_rsem.at[n, d], core)

    def c_copy(seg):
        blk = kvg.at[:, rows(seg, c)]
        return remote(blk, blk, c_ssem.at[seg], c_rsem.at[seg], core)

    def c_arrival(seg):
        blk = kvg.at[:, rows(seg, 1 - c)]
        return remote(blk, blk, c_ssem.at[seg], c_rsem.at[seg], core)

    for t in range(2):
        kv_local(t).start()
        for d in (1, 3, 2):
            kv_copy(t, d).start()
    for t in range(2):
        q_local(t).start()
        q_copy(t, 0, 1).start()

    def send_next(d):
        @pl.when(has_next)
        def _():
            x_copy(1, d).start()
            x_copy(2, d).start()

    for t in range(2):
        kv_local(t).wait()
    x_copy(0, 0).start()
    send_next(0)
    def pk_row(blk, value):
        pk[blk] = value

    lane = lax.broadcasted_iota(jnp.int32, (8, TOK), 1)
    for xx in range(2):
        for cc in range(2):
            for yy in range(4):
                first = 2 * (yy * 4 + xx * 2 + cc)
                span = jnp.where(lane < 64, span_ref[first], span_ref[first + 1])
                blk = jnp.where(xl == xx, 0, 8) + cc * 4 + yy
                pk_row(blk, (span * 64 + lax.rem(lane, 64)).astype(F32))
    for blk in range(16, 32):
        pk_row(blk, jnp.full((8, TOK), -1.0, F32))
    sub = lax.broadcasted_iota(jnp.int32, (64, 128), 0)
    for rel in range(4):
        for cc in range(2):
            for hb in range(2):
                span = span_ref[2 * (yrel(rel) * 4 + xl * 2 + cc) + hb]
                at = (cc * 2 + hb) * 64
                pq[rel, at : at + 64, :] = (span * 64 + sub).astype(F32)

    dka[...] = jnp.zeros_like(dka)
    dva[...] = jnp.zeros_like(dva)

    for d in (3, 1, 2):
        for t in range(2):
            kv_copy(t, 4 - d).wait_recv()
        x_copy(0, d).start()
    for d in (3, 1):
        for dc in range(2):
            for t in range(2):
                q_copy(t, d, dc).start()
    for d in (3, 1, 2):
        send_next(d)
    c_copy(0).start()
    c_arrival(0).wait_recv()
    for d in range(4):
        x_arrival(0, d).wait_recv()
    c_copy(1).start()
    for t in range(2):
        q_local(t).wait()
        q_copy(t, 0, 1).wait_recv()
    c_arrival(1).wait_recv()

    def take_previous():
        for n in (1, 2):
            for d in range(4):
                x_arrival(n, d).wait_recv()
            c_copy(1 + n).start()
        for n in (1, 2):
            c_arrival(1 + n).wait_recv()

    mine = pl.ds(pl.multiple_of((y * 2 + c) * COLS, 128), COLS)

    def dq_copy(r, dc):
        cc = 1 - c if dc else c
        src = dqs.at[r, pl.ds(pl.multiple_of(cc * TOK, TOK), TOK)]
        return remote(
            src,
            gq_ref.at[:, mine],
            dq_ssem.at[r, dc],
            dq_rsem.at[lax.rem(4 - r, 4), dc],
            dev(o, yrel(r), xl, cc),
        )

    def dq_arrival(r, dc):
        cc = 1 - c if dc else c
        dst = gq_ref.at[:, pl.ds(pl.multiple_of((yrel(r) * 2 + cc) * COLS, 128), COLS)]
        return remote(dst, dst, dq_ssem.at[0, 1], dq_rsem.at[r, dc], core)

    dq_local = pltpu.make_async_copy(
        dqs.at[0, pl.ds(pl.multiple_of(c * TOK, TOK), TOK)], gq_ref.at[:, mine], l_sem.at[4]
    )

    acc = (dka, dva)

    def rc_copy(seg):
        return remote(cx.at[seg], rx.at[seg], rc_ssem.at[seg], rc_rsem.at[seg], core)

    def rx_copy(n):
        if n == 0:
            return remote(xs.at[0], xr.at[0], rx_ssem.at[0], rx_rsem.at[0], dev(o, y, 1 - xl, c))
        return remote(xs.at[n], xr.at[1 + xl], rx_ssem.at[n], rx_rsem.at[1 + xl], dev(o_prev, y, n - 1, c))

    def rx_arrival(n):
        return remote(xr.at[n], xr.at[n], rx_ssem.at[0], rx_rsem.at[n], core)

    def ry_copy(d):
        yy = yrel(d)
        return remote(ys.at[yy], yr.at[y], ry_ssem.at[d - 1], ry_rsem.at[3 - d], dev(o, yy, xl, c))

    def ry_arrival(r):
        dst = yr.at[yrel(r)]
        return remote(dst, dst, ry_ssem.at[0], ry_rsem.at[r - 1], core)

    def send_core(seg):
        def step(yy, _):
            for t in range(2):
                cx[seg, t, yy] = acc[t][seg * 8 + (1 - c) * 4 + yy].astype(BF16)
            return 0

        lax.fori_loop(0, 4, step, 0)
        rc_copy(seg).start()

    def send_x(seg):
        rc_copy(seg).wait_recv()

        def step(yy, _):
            for t in range(2):
                xs[seg - 1, t, yy] = (acc[t][seg * 8 + c * 4 + yy] + rx[seg, t, yy].astype(F32)).astype(BF16)
            return 0

        lax.fori_loop(0, 4, step, 0)
        rx_copy(seg - 1).start()

    nl = SEG // 128
    hrows = [slice(h * SET, h * SET + SET) for h in range(NH)]
    hcols = [slice(h * HEAD, h * HEAD + HEAD) for h in range(NH)]

    def lanes(j):
        return slice(j * 128, j * 128 + 128)

    def keys_of(t, seg):
        return kvg[t, seg * SEG : seg * SEG + SEG, :]

    def scores(rel, first, masked):
        for half in range(2):
            keys = keys_of(0, first + half)
            for h in range(NH):
                r = hrows[h]
                s = lax.dot_general(qraw[rel, :, hcols[h]], keys, NT, preferred_element_type=F32)
                m = mx[r, :]
                for j in range(nl):
                    sj = s[:, lanes(j)] * SCALE2
                    if masked:
                        sj = jnp.where(pk[(first + half) * nl + j, 0:1, :] <= pq[rel], sj, MASKED)
                    m = jnp.maximum(m, sj)
                    s_buf[half, r, lanes(j)] = sj
                mx[r, :] = m

    def weights(rel, first):
        for half in range(2):
            vals = keys_of(1, first + half)
            for h in range(NH):
                dp = lax.dot_general(doraw[rel, :, hcols[h]], vals, NT, preferred_element_type=F32)
                for g0 in range(0, SET, VR):
                    g = slice(h * SET + g0, h * SET + g0 + VR)
                    m, l, d = mx[g, :], st_l[rel, g, :], st_d[rel, g, :]
                    for j in range(nl):
                        e = jnp.exp2(s_buf[half, g, lanes(j)] - m)
                        dpj = dp[g0 : g0 + VR, lanes(j)]
                        l = l + e
                        d = d + e * dpj
                        e_buf[first + half, rel, g, lanes(j)] = e.astype(BF16)
                    st_l[rel, g, :] = l
                    st_d[rel, g, :] = d

    def scaled_t(x, w):
        return (x.astype(F32) * w).astype(BF16).T

    def own_keys(rel):
        @pl.when(rel > 0)
        def _():
            for dc in range(2):
                for t in range(2):
                    q_copy(t, 4 - rel, dc).wait_recv()

        mx[...] = jnp.full(mx.shape, MASKED, F32)
        st_l[rel] = jnp.zeros((ROWS, 128), F32)
        st_d[rel] = jnp.zeros((ROWS, 128), F32)
        dqp[rel] = jnp.zeros((ROWS, HEAD), F32)
        scores(rel, 0, True)
        for r in hrows:
            m = jnp.broadcast_to(jnp.max(mx[r, :], axis=1, keepdims=True), (SET, 128))
            mx[r, :] = m
            wgt[0, rel, r, :] = m
        weights(rel, 0)

    def previous_keys(rel):
        @pl.when(has_prev)
        def _():
            mx[...] = jnp.full(mx.shape, MASKED, F32)
            scores(rel, 2, False)
            for r in hrows:
                top = jnp.max(mx[r, :], axis=1, keepdims=True)
                before = wgt[0, rel, r, :]
                m = jnp.maximum(before, top)
                shrink = jnp.exp2(before - m)
                mx[r, :] = m
                wgt[0, rel, r, :] = shrink
                st_l[rel, r, :] = st_l[rel, r, :] * shrink
                st_d[rel, r, :] = st_d[rel, r, :] * shrink
            weights(rel, 2)

        @pl.when(jnp.logical_not(has_prev))
        def _():
            wgt[0, rel] = jnp.ones((ROWS, 128), F32)

        for h in range(NH):
            r = hrows[h]
            rinv = 1.0 / jnp.sum(st_l[rel, r, :], axis=1, keepdims=True)
            delta = jnp.sum(st_d[rel, r, :], axis=1, keepdims=True) * rinv
            st_d[rel, r, :] = jnp.broadcast_to(delta, (SET, 128))
            factors = (wgt[0, rel, r, :] * rinv, jnp.broadcast_to(rinv, (SET, 128)))
            for g in range(2):
                wgt[g, rel, r, :] = factors[g]
                qt[g, rel, :, r] = scaled_t(qraw[rel, :, hcols[h]], factors[g])
                dot[g, rel, :, r] = scaled_t(doraw[rel, :, hcols[h]], factors[g])

    def forward(step, _):
        t = jnp.where(step >= 3, step - 3, step)
        rel = jnp.where(step >= 6, 2, jnp.where(t == 2, 3, t))
        own = (step < 3) | (step == 6)

        @pl.when(step == 1)
        def _():
            for dc in range(2):
                for t in range(2):
                    q_copy(t, 2, dc).start()

        @pl.when((step == 3) & has_prev)
        def _():
            take_previous()

        @pl.when(own)
        def _():
            own_keys(rel)

        @pl.when(jnp.logical_not(own))
        def _():
            previous_keys(rel)

        return 0

    lax.fori_loop(0, 8, forward, 0)

    def gradients(it, _):
        order = it // 4
        seg = jnp.where(order < 2, order + 2, 3 - order)
        rel = lax.rem(it + 1, 4)
        grp = jnp.where(order < 2, 1, 0)

        for at, event, n in ((4, send_core, 2), (6, send_x, 2), (8, send_core, 3), (10, send_x, 3)):

            @pl.when((it == at) & has_prev)
            def _(event=event, n=n):
                event(n)

        @pl.when(it == 12)
        def _():
            send_core(1)

        @pl.when(it == 14)
        def _():
            send_x(1)

        at = pl.ds(pl.multiple_of(seg * SEG, SEG), SEG)
        keys, vals = kvg[0, at, :], kvg[1, at, :]
        dv = jnp.dot(dot[grp, rel], e_buf[seg, rel], preferred_element_type=F32)
        dk = None
        for h in range(NH):
            r = hrows[h]
            dp = lax.dot_general(doraw[rel, :, hcols[h]], vals, NT, preferred_element_type=F32)
            parts = []
            for g0 in range(0, SET, VR):
                g = slice(h * SET + g0, h * SET + g0 + VR)
                d = st_d[rel, g, :]
                part = []
                for j in range(nl):
                    e = e_buf[seg, rel, g, lanes(j)].astype(F32)
                    part.append((e * (dp[g0 : g0 + VR, lanes(j)] - d)).astype(BF16))
                parts.append(jnp.concatenate(part, axis=1))
            ds = jnp.concatenate(parts, axis=0)
            dqp[rel, r, :] += jnp.dot(ds, keys, preferred_element_type=F32) * (wgt[grp, rel, r, :] * SCALE)
            part = jnp.dot(qt[grp, rel, :, r], ds, preferred_element_type=F32)
            dk = part if dk is None else dk + part
        for j in range(nl):
            dva[seg * nl + j] += dv[:, lanes(j)]
            dka[seg * nl + j] += dk[:, lanes(j)]

        @pl.when(seg == 0)
        def _():
            for h in range(NH):
                dqs[rel, :, hcols[h]] = dqp[rel, hrows[h], :].astype(BF16)

            @pl.when(rel > 0)
            def _():
                dq_copy(rel, 0).start()

            @pl.when(rel == 0)
            def _():
                dq_local.start()

            dq_copy(rel, 1).start()

        return 0

    lax.fori_loop(jnp.where(has_prev, 0, 8), 16, gradients, 0)
    send_core(0)
    rc_copy(0).wait_recv()

    def own(yy, _):
        for t in range(2):
            blk = c * 4 + yy
            acc[t][blk] = acc[t][blk] + rx[0, t, yy].astype(F32)
        return 0

    lax.fori_loop(0, 4, own, 0)

    def take(n):
        rx_arrival(n).wait_recv()

        def step(yy, _):
            for t in range(2):
                blk = c * 4 + yy
                acc[t][blk] = acc[t][blk] + xr[n, t, yy].astype(F32)
            return 0

        lax.fori_loop(0, 4, step, 0)

    take(0)

    @pl.when(has_next)
    def _():
        take(1)
        take(2)

    def final(yy, _):
        blk = c * 4 + yy
        ys[yy, 0] = (acc[0][blk] * SCALE).astype(BF16)
        ys[yy, 1] = acc[1][blk].astype(BF16)
        return 0

    lax.fori_loop(0, 4, final, 0)
    for d in range(1, 4):
        ry_copy(d).start()
    outs = (gk_ref, gv_ref)
    at_me = pl.ds(pl.multiple_of(y * HEAD, HEAD), HEAD)
    for t in range(2):
        outs[t][:, at_me] = ys[y, t].T
    for r in range(1, 4):
        ry_arrival(r).wait_recv()
        at = pl.ds(pl.multiple_of(yrel(r) * HEAD, HEAD), HEAD)
        for t in range(2):
            outs[t][:, at] = yr[yrel(r), t].T

    dq_local.wait()
    for r in range(4):
        for dc in range(2):
            if r or dc:
                dq_arrival(r, dc).wait_recv()
                dq_copy(r, dc).wait_send()
                for t in range(2):
                    q_copy(t, r, dc).wait_send()
    for d in range(1, 4):
        ry_copy(d).wait_send()
        for t in range(2):
            kv_copy(t, d).wait_send()
    for d in range(4):
        x_copy(0, d).wait_send()
    rx_copy(0).wait_send()
    for seg in range(2):
        c_copy(seg).wait_send()
        rc_copy(seg).wait_send()

    @pl.when(has_next)
    def _():
        for d in range(4):
            x_copy(1, d).wait_send()
            x_copy(2, d).wait_send()

    @pl.when(has_prev)
    def _():
        for seg in (2, 3):
            c_copy(seg).wait_send()
            rc_copy(seg).wait_send()
            rx_copy(seg - 1).wait_send()


def hand_over(a0, a1, a2, b0, b1, b2):
    b0[...] = a0[...]
    b1[...] = a1[...]
    b2[...] = a2[...]


def on_device(queries, keys, values, output_gradient, span_order):
    vmem = pl.BlockSpec(memory_space=pltpu.VMEM)
    hbm = pl.BlockSpec(memory_space=pl.ANY)
    dma = pltpu.SemaphoreType.DMA
    results = pl.pallas_call(
        kernel,
        out_shape=[
            jax.ShapeDtypeStruct(queries.shape, BF16),
            jax.ShapeDtypeStruct(keys.shape, BF16),
            jax.ShapeDtypeStruct(values.shape, BF16),
        ],
        in_specs=[hbm, vmem, vmem, hbm, pl.BlockSpec(memory_space=pltpu.SMEM)],
        out_specs=[hbm, vmem, vmem],
        scratch_shapes=[
            pltpu.VMEM((4, SET, COLS), BF16),
            pltpu.VMEM((4, SET, COLS), BF16),
            pltpu.VMEM((2, NKEY, HEAD), BF16),
            pltpu.VMEM((32, 8, TOK), F32),
            pltpu.VMEM((4, SET, 128), F32),
            pltpu.VMEM((2, 4, HEAD, ROWS), BF16),
            pltpu.VMEM((2, 4, HEAD, ROWS), BF16),
            pltpu.VMEM((2, ROWS, SEG), F32),
            pltpu.VMEM((4, 4, ROWS, SEG), BF16),
            pltpu.VMEM((ROWS, 128), F32),
            pltpu.VMEM((2, 4, ROWS, 128), F32),
            pltpu.VMEM((4, ROWS, 128), F32),
            pltpu.VMEM((4, ROWS, 128), F32),
            pltpu.VMEM((4, ROWS, HEAD), F32),
            pltpu.VMEM((32, HEAD, 128), F32),
            pltpu.VMEM((32, HEAD, 128), F32),
            pltpu.VMEM((4, SET, COLS), BF16),
            pltpu.VMEM((4, 2, 4, HEAD, 128), BF16),
            pltpu.VMEM((4, 2, 4, HEAD, 128), BF16),
            pltpu.VMEM((3, 2, 4, HEAD, 128), BF16),
            pltpu.VMEM((3, 2, 4, HEAD, 128), BF16),
            pltpu.VMEM((4, 2, HEAD, 128), BF16),
            pltpu.VMEM((4, 2, HEAD, 128), BF16),
            dma((2, 4, 2)), dma((2, 4, 2)),
            dma((2, 3)), dma((2, 3)),
            dma((3, 4)), dma((3, 4)),
            dma((4,)), dma((4,)),
            dma((5,)),
            dma((4, 2)), dma((4, 2)),
            dma((4,)), dma((4,)),
            dma((3,)), dma((3,)),
            dma((3,)), dma((3,)),
        ],
        compiler_params=pltpu.CompilerParams(
            collective_id=0, has_side_effects=True, vmem_limit_bytes=62 * 2**20
        ),
        name="attention_backward",
    )(queries, keys, values, output_gradient, span_order)
    parts = 2
    blocks = [pl.BlockSpec((x.shape[0] // parts, x.shape[1]), lambda n: (n, 0)) for x in results]
    return pl.pallas_call(
        hand_over,
        grid=(parts,),
        out_shape=[jax.ShapeDtypeStruct(x.shape, BF16) for x in results],
        in_specs=blocks,
        out_specs=blocks,
        compiler_params=pltpu.CompilerParams(vmem_limit_bytes=62 * 2**20),
        name="hand_over",
    )(*results)


def solution(mesh):
    rows = P(("outer", "inner"), None)
    return jax.shard_map(
        on_device,
        mesh=mesh,
        in_specs=(rows, rows, rows, rows, P()),
        out_specs=(rows, rows, rows),
        check_vma=False,
    )
```

```python
import jax
import jax.numpy as jnp
from jax import lax
from jax.experimental import pallas as pl
from jax.experimental.pallas import tpu as pltpu
from jax.sharding import PartitionSpec as P

MESH = pl.DeviceIdType.MESH
F32 = jnp.float32
BF16 = jnp.bfloat16
SCALE = 128**-0.5
SCALE2 = SCALE * 1.4426950408889634
MASKED = -1.0e30
NT = (((1,), (1,)), ((), ()))

HEAD = 128
TOK = 128
NH = 3
SET = 2 * TOK
ROWS = NH * SET
COLS = NH * HEAD
SEG = 8 * TOK
NKEY = 4 * SEG
VR = 16


def kernel(
    q_ref, k_ref, v_ref, do_ref, span_ref,
    gq_ref, gk_ref, gv_ref,
    qraw, doraw, kvg, pk, pq, qt, dot, s_buf, e_buf, mx, wgt, st_l, st_d, dqp, dka, dva, dqs,
    cx, rx, xs, xr, ys, yr,
    q_ssem, q_rsem, y_ssem, y_rsem, x_ssem, x_rsem, c_ssem, c_rsem, l_sem,
    dq_ssem, dq_rsem, rc_ssem, rc_rsem, rx_ssem, rx_rsem, ry_ssem, ry_rsem,
):
    o = lax.axis_index("outer")
    i = lax.axis_index("inner")
    y, xl, c = i // 4, (i // 2) % 2, i % 2
    has_prev = o > 0
    has_next = o < 7

    def dev(oo, yy, xx, cc):
        return (oo, yy * 4 + xx * 2 + cc)

    def yrel(d):
        return lax.rem(y + d, 4)

    def remote(src, dst, ssem, rsem, device):
        return pltpu.make_async_remote_copy(
            src_ref=src, dst_ref=dst, send_sem=ssem, recv_sem=rsem, device_id=device, device_id_type=MESH
        )

    o_next, o_prev = lax.rem(o + 1, 8), lax.rem(o + 7, 8)
    core = dev(o, y, xl, 1 - c)

    barrier = pltpu.get_barrier_semaphore()
    peers = [dev(o, yrel(d), xl, cc) for d in range(1, 4) for cc in range(2)]
    peers += [core, dev(o, y, 1 - xl, c)]
    peers += [dev(oo, y, xx, c) for oo in (o_next, o_prev) for xx in range(2)]
    for p in peers:
        pl.semaphore_signal(barrier, inc=1, device_id=p, device_id_type=MESH)
    pl.semaphore_wait(barrier, len(peers))

    def rows(seg, cc, yy=0, n=4):
        return pl.ds(pl.multiple_of(seg * SEG + cc * 4 * TOK + yy * TOK, TOK), n * TOK)

    def kv_copy(t, d):
        yy = yrel(d)
        src = (k_ref, v_ref)[t].at[:, pl.ds(pl.multiple_of(yy * HEAD, HEAD), HEAD)]
        return remote(src, kvg.at[t, rows(0, c, y, 1)], y_ssem.at[t, d - 1], y_rsem.at[t, 3 - d], dev(o, yy, xl, c))

    def kv_local(t):
        src = (k_ref, v_ref)[t].at[:, pl.ds(pl.multiple_of(y * HEAD, HEAD), HEAD)]
        return pltpu.make_async_copy(src, kvg.at[t, rows(0, c, y, 1)], l_sem.at[t])

    def q_copy(t, d, dc):
        yy, cc = yrel(d), (1 - c if dc else c)
        src = (q_ref, do_ref)[t].at[:, pl.ds(pl.multiple_of((yy * 2 + cc) * COLS, 128), COLS)]
        r = lax.rem(4 - d, 4)
        dst = (qraw, doraw)[t].at[r, pl.ds(pl.multiple_of(c * TOK, TOK), TOK)]
        return remote(src, dst, q_ssem.at[t, d, dc], q_rsem.at[t, r, dc], dev(o, yy, xl, cc))

    def q_local(t):
        src = (q_ref, do_ref)[t].at[:, pl.ds(pl.multiple_of((y * 2 + c) * COLS, 128), COLS)]
        dst = (qraw, doraw)[t].at[0, pl.ds(pl.multiple_of(c * TOK, TOK), TOK)]
        return pltpu.make_async_copy(src, dst, l_sem.at[2 + t])

    def x_copy(n, d):
        yy = yrel(d)
        src = kvg.at[:, rows(0, c, yy, 1)]
        if n == 0:
            dst, device, slot = kvg.at[:, rows(1, c, yy, 1)], dev(o, y, 1 - xl, c), 0
        else:
            dst, device, slot = kvg.at[:, rows(2 + xl, c, yy, 1)], dev(o_next, y, n - 1, c), 1 + xl
        return remote(src, dst, x_ssem.at[n, d], x_rsem.at[slot, d], device)

    def x_arrival(n, d):
        dst = kvg.at[:, rows(1 + n, c, yrel(d), 1)]
        return remote(dst, dst, x_ssem.at[0, 0], x_rsem.at[n, d], core)

    def c_copy(seg):
        blk = kvg.at[:, rows(seg, c)]
        return remote(blk, blk, c_ssem.at[seg], c_rsem.at[seg], core)

    def c_arrival(seg):
        blk = kvg.at[:, rows(seg, 1 - c)]
        return remote(blk, blk, c_ssem.at[seg], c_rsem.at[seg], core)

    for t in range(2):
        kv_local(t).start()
        for d in (1, 3, 2):
            kv_copy(t, d).start()
    for t in range(2):
        q_local(t).start()
        q_copy(t, 0, 1).start()

    def send_next(d):
        @pl.when(has_next)
        def _():
            x_copy(1, d).start()
            x_copy(2, d).start()

    for t in range(2):
        kv_local(t).wait()
    x_copy(0, 0).start()
    send_next(0)
    def pk_row(blk, value):
        pk[blk] = value

    lane = lax.broadcasted_iota(jnp.int32, (8, TOK), 1)
    for xx in range(2):
        for cc in range(2):
            for yy in range(4):
                first = 2 * (yy * 4 + xx * 2 + cc)
                span = jnp.where(lane < 64, span_ref[first], span_ref[first + 1])
                blk = jnp.where(xl == xx, 0, 8) + cc * 4 + yy
                pk_row(blk, (span * 64 + lax.rem(lane, 64)).astype(F32))
    for blk in range(16, 32):
        pk_row(blk, jnp.full((8, TOK), -1.0, F32))
    sub = lax.broadcasted_iota(jnp.int32, (64, 128), 0)
    for rel in range(4):
        for cc in range(2):
            for hb in range(2):
                span = span_ref[2 * (yrel(rel) * 4 + xl * 2 + cc) + hb]
                at = (cc * 2 + hb) * 64
                pq[rel, at : at + 64, :] = (span * 64 + sub).astype(F32)

    dka[...] = jnp.zeros_like(dka)
    dva[...] = jnp.zeros_like(dva)

    for d in (3, 1, 2):
        for t in range(2):
            kv_copy(t, 4 - d).wait_recv()
        x_copy(0, d).start()
    for d in (3, 1):
        for dc in range(2):
            for t in range(2):
                q_copy(t, d, dc).start()
    for d in (3, 1, 2):
        send_next(d)
    c_copy(0).start()
    c_arrival(0).wait_recv()
    for d in range(4):
        x_arrival(0, d).wait_recv()
    c_copy(1).start()
    for t in range(2):
        q_local(t).wait()
        q_copy(t, 0, 1).wait_recv()
    c_arrival(1).wait_recv()

    def take_previous():
        for n in (1, 2):
            for d in range(4):
                x_arrival(n, d).wait_recv()
            c_copy(1 + n).start()
        for n in (1, 2):
            c_arrival(1 + n).wait_recv()

    mine = pl.ds(pl.multiple_of((y * 2 + c) * COLS, 128), COLS)

    def dq_copy(r, dc):
        cc = 1 - c if dc else c
        src = dqs.at[r, pl.ds(pl.multiple_of(cc * TOK, TOK), TOK)]
        return remote(
            src,
            gq_ref.at[:, mine],
            dq_ssem.at[r, dc],
            dq_rsem.at[lax.rem(4 - r, 4), dc],
            dev(o, yrel(r), xl, cc),
        )

    def dq_arrival(r, dc):
        cc = 1 - c if dc else c
        dst = gq_ref.at[:, pl.ds(pl.multiple_of((yrel(r) * 2 + cc) * COLS, 128), COLS)]
        return remote(dst, dst, dq_ssem.at[0, 1], dq_rsem.at[r, dc], core)

    dq_local = pltpu.make_async_copy(
        dqs.at[0, pl.ds(pl.multiple_of(c * TOK, TOK), TOK)], gq_ref.at[:, mine], l_sem.at[4]
    )

    acc = (dka, dva)

    def rc_copy(seg):
        return remote(cx.at[seg], rx.at[seg], rc_ssem.at[seg], rc_rsem.at[seg], core)

    def rx_copy(n):
        if n == 0:
            return remote(xs.at[0], xr.at[0], rx_ssem.at[0], rx_rsem.at[0], dev(o, y, 1 - xl, c))
        return remote(xs.at[n], xr.at[1 + xl], rx_ssem.at[n], rx_rsem.at[1 + xl], dev(o_prev, y, n - 1, c))

    def rx_arrival(n):
        return remote(xr.at[n], xr.at[n], rx_ssem.at[0], rx_rsem.at[n], core)

    def ry_copy(d):
        yy = yrel(d)
        return remote(ys.at[yy], yr.at[y], ry_ssem.at[d - 1], ry_rsem.at[3 - d], dev(o, yy, xl, c))

    def ry_arrival(r):
        dst = yr.at[yrel(r)]
        return remote(dst, dst, ry_ssem.at[0], ry_rsem.at[r - 1], core)

    def send_core(seg):
        def step(yy, _):
            for t in range(2):
                cx[seg, t, yy] = acc[t][seg * 8 + (1 - c) * 4 + yy].astype(BF16)
            return 0

        lax.fori_loop(0, 4, step, 0)
        rc_copy(seg).start()

    def send_x(seg):
        rc_copy(seg).wait_recv()

        def step(yy, _):
            for t in range(2):
                xs[seg - 1, t, yy] = (acc[t][seg * 8 + c * 4 + yy] + rx[seg, t, yy].astype(F32)).astype(BF16)
            return 0

        lax.fori_loop(0, 4, step, 0)
        rx_copy(seg - 1).start()

    nl = SEG // 128
    hrows = [slice(h * SET, h * SET + SET) for h in range(NH)]
    hcols = [slice(h * HEAD, h * HEAD + HEAD) for h in range(NH)]

    def lanes(j):
        return slice(j * 128, j * 128 + 128)

    def keys_of(t, seg):
        return kvg[t, seg * SEG : seg * SEG + SEG, :]

    def scores(rel, first, masked):
        for half in range(2):
            keys = keys_of(0, first + half)
            for h in range(NH):
                r = hrows[h]
                s = lax.dot_general(qraw[rel, :, hcols[h]], keys, NT, preferred_element_type=F32)
                m = mx[r, :]
                for j in range(nl):
                    sj = s[:, lanes(j)] * SCALE2
                    if masked:
                        sj = jnp.where(pk[(first + half) * nl + j, 0:1, :] <= pq[rel], sj, MASKED)
                    m = jnp.maximum(m, sj)
                    s_buf[half, r, lanes(j)] = sj
                mx[r, :] = m

    def weights(rel, first):
        for half in range(2):
            vals = keys_of(1, first + half)
            for h in range(NH):
                dp = lax.dot_general(doraw[rel, :, hcols[h]], vals, NT, preferred_element_type=F32)
                for g0 in range(0, SET, VR):
                    g = slice(h * SET + g0, h * SET + g0 + VR)
                    m, l, d = mx[g, :], st_l[rel, g, :], st_d[rel, g, :]
                    for j in range(nl):
                        e = jnp.exp2(s_buf[half, g, lanes(j)] - m)
                        dpj = dp[g0 : g0 + VR, lanes(j)]
                        l = l + e
                        d = d + e * dpj
                        e_buf[first + half, rel, g, lanes(j)] = e.astype(BF16)
                    st_l[rel, g, :] = l
                    st_d[rel, g, :] = d

    def scaled_t(x, w):
        return (x.astype(F32) * w).astype(BF16).T

    def own_keys(rel):
        @pl.when(rel > 0)
        def _():
            for dc in range(2):
                for t in range(2):
                    q_copy(t, 4 - rel, dc).wait_recv()

        mx[...] = jnp.full(mx.shape, MASKED, F32)
        st_l[rel] = jnp.zeros((ROWS, 128), F32)
        st_d[rel] = jnp.zeros((ROWS, 128), F32)
        dqp[rel] = jnp.zeros((ROWS, HEAD), F32)
        scores(rel, 0, True)
        for r in hrows:
            m = jnp.broadcast_to(jnp.max(mx[r, :], axis=1, keepdims=True), (SET, 128))
            mx[r, :] = m
            wgt[0, rel, r, :] = m
        weights(rel, 0)

    def previous_keys(rel):
        @pl.when(has_prev)
        def _():
            mx[...] = jnp.full(mx.shape, MASKED, F32)
            scores(rel, 2, False)
            for r in hrows:
                top = jnp.max(mx[r, :], axis=1, keepdims=True)
                before = wgt[0, rel, r, :]
                m = jnp.maximum(before, top)
                shrink = jnp.exp2(before - m)
                mx[r, :] = m
                wgt[0, rel, r, :] = shrink
                st_l[rel, r, :] = st_l[rel, r, :] * shrink
                st_d[rel, r, :] = st_d[rel, r, :] * shrink
            weights(rel, 2)

        @pl.when(jnp.logical_not(has_prev))
        def _():
            wgt[0, rel] = jnp.ones((ROWS, 128), F32)

        for h in range(NH):
            r = hrows[h]
            rinv = 1.0 / jnp.sum(st_l[rel, r, :], axis=1, keepdims=True)
            delta = jnp.sum(st_d[rel, r, :], axis=1, keepdims=True) * rinv
            st_d[rel, r, :] = jnp.broadcast_to(delta, (SET, 128))
            factors = (wgt[0, rel, r, :] * rinv, jnp.broadcast_to(rinv, (SET, 128)))
            for g in range(2):
                wgt[g, rel, r, :] = factors[g]
                qt[g, rel, :, r] = scaled_t(qraw[rel, :, hcols[h]], factors[g])
                dot[g, rel, :, r] = scaled_t(doraw[rel, :, hcols[h]], factors[g])

    def forward(step, _):
        t = jnp.where(step >= 3, step - 3, step)
        rel = jnp.where(step >= 6, 2, jnp.where(t == 2, 3, t))
        own = (step < 3) | (step == 6)

        @pl.when(step == 1)
        def _():
            for dc in range(2):
                for t in range(2):
                    q_copy(t, 2, dc).start()

        @pl.when((step == 3) & has_prev)
        def _():
            take_previous()

        @pl.when(own)
        def _():
            own_keys(rel)

        @pl.when(jnp.logical_not(own))
        def _():
            previous_keys(rel)

        return 0

    lax.fori_loop(0, 8, forward, 0)

    def gradients(it, _):
        order = it // 4
        seg = jnp.where(order < 2, order + 2, 3 - order)
        rel = lax.rem(it + 1, 4)
        grp = jnp.where(order < 2, 1, 0)

        for at, event, n in ((4, send_core, 2), (6, send_x, 2), (8, send_core, 3), (10, send_x, 3)):

            @pl.when((it == at) & has_prev)
            def _(event=event, n=n):
                event(n)

        @pl.when(it == 12)
        def _():
            send_core(1)

        @pl.when(it == 14)
        def _():
            send_x(1)

        at = pl.ds(pl.multiple_of(seg * SEG, SEG), SEG)
        keys, vals = kvg[0, at, :], kvg[1, at, :]
        dk = None
        for h in range(NH):
            r = hrows[h]
            dp = lax.dot_general(doraw[rel, :, hcols[h]], vals, NT, preferred_element_type=F32)
            parts = []
            for g0 in range(0, SET, VR):
                g = slice(h * SET + g0, h * SET + g0 + VR)
                d = st_d[rel, g, :]
                part = []
                for j in range(nl):
                    e = e_buf[seg, rel, g, lanes(j)].astype(F32)
                    part.append((e * (dp[g0 : g0 + VR, lanes(j)] - d)).astype(BF16))
                parts.append(jnp.concatenate(part, axis=1))
            ds = jnp.concatenate(parts, axis=0)
            dqp[rel, r, :] += jnp.dot(ds, keys, preferred_element_type=F32) * (wgt[grp, rel, r, :] * SCALE)
            part = jnp.dot(qt[grp, rel, :, r], ds, preferred_element_type=F32)
            dk = part if dk is None else dk + part
        dv = jnp.dot(dot[grp, rel], e_buf[seg, rel], preferred_element_type=F32)
        for j in range(nl):
            dva[seg * nl + j] += dv[:, lanes(j)]
            dka[seg * nl + j] += dk[:, lanes(j)]

        @pl.when(seg == 0)
        def _():
            for h in range(NH):
                dqs[rel, :, hcols[h]] = dqp[rel, hrows[h], :].astype(BF16)

            @pl.when(rel > 0)
            def _():
                dq_copy(rel, 0).start()

            @pl.when(rel == 0)
            def _():
                dq_local.start()

            dq_copy(rel, 1).start()

        return 0

    lax.fori_loop(jnp.where(has_prev, 0, 8), 16, gradients, 0)
    send_core(0)
    rc_copy(0).wait_recv()

    def own(yy, _):
        for t in range(2):
            blk = c * 4 + yy
            acc[t][blk] = acc[t][blk] + rx[0, t, yy].astype(F32)
        return 0

    lax.fori_loop(0, 4, own, 0)

    def take(n):
        rx_arrival(n).wait_recv()

        def step(yy, _):
            for t in range(2):
                blk = c * 4 + yy
                acc[t][blk] = acc[t][blk] + xr[n, t, yy].astype(F32)
            return 0

        lax.fori_loop(0, 4, step, 0)

    take(0)

    @pl.when(has_next)
    def _():
        take(1)
        take(2)

    def final(yy, _):
        blk = c * 4 + yy
        ys[yy, 0] = (acc[0][blk] * SCALE).astype(BF16)
        ys[yy, 1] = acc[1][blk].astype(BF16)
        return 0

    lax.fori_loop(0, 4, final, 0)
    for d in range(1, 4):
        ry_copy(d).start()
    outs = (gk_ref, gv_ref)
    at_me = pl.ds(pl.multiple_of(y * HEAD, HEAD), HEAD)
    for t in range(2):
        outs[t][:, at_me] = ys[y, t].T
    for r in range(1, 4):
        ry_arrival(r).wait_recv()
        at = pl.ds(pl.multiple_of(yrel(r) * HEAD, HEAD), HEAD)
        for t in range(2):
            outs[t][:, at] = yr[yrel(r), t].T

    dq_local.wait()
    for r in range(4):
        for dc in range(2):
            if r or dc:
                dq_arrival(r, dc).wait_recv()
                dq_copy(r, dc).wait_send()
                for t in range(2):
                    q_copy(t, r, dc).wait_send()
    for d in range(1, 4):
        ry_copy(d).wait_send()
        for t in range(2):
            kv_copy(t, d).wait_send()
    for d in range(4):
        x_copy(0, d).wait_send()
    rx_copy(0).wait_send()
    for seg in range(2):
        c_copy(seg).wait_send()
        rc_copy(seg).wait_send()

    @pl.when(has_next)
    def _():
        for d in range(4):
            x_copy(1, d).wait_send()
            x_copy(2, d).wait_send()

    @pl.when(has_prev)
    def _():
        for seg in (2, 3):
            c_copy(seg).wait_send()
            rc_copy(seg).wait_send()
            rx_copy(seg - 1).wait_send()


def hand_over(a0, a1, a2, b0, b1, b2):
    b0[...] = a0[...]
    b1[...] = a1[...]
    b2[...] = a2[...]


def on_device(queries, keys, values, output_gradient, span_order):
    vmem = pl.BlockSpec(memory_space=pltpu.VMEM)
    hbm = pl.BlockSpec(memory_space=pl.ANY)
    dma = pltpu.SemaphoreType.DMA
    results = pl.pallas_call(
        kernel,
        out_shape=[
            jax.ShapeDtypeStruct(queries.shape, BF16),
            jax.ShapeDtypeStruct(keys.shape, BF16),
            jax.ShapeDtypeStruct(values.shape, BF16),
        ],
        in_specs=[hbm, vmem, vmem, hbm, pl.BlockSpec(memory_space=pltpu.SMEM)],
        out_specs=[hbm, vmem, vmem],
        scratch_shapes=[
            pltpu.VMEM((4, SET, COLS), BF16),
            pltpu.VMEM((4, SET, COLS), BF16),
            pltpu.VMEM((2, NKEY, HEAD), BF16),
            pltpu.VMEM((32, 8, TOK), F32),
            pltpu.VMEM((4, SET, 128), F32),
            pltpu.VMEM((2, 4, HEAD, ROWS), BF16),
            pltpu.VMEM((2, 4, HEAD, ROWS), BF16),
            pltpu.VMEM((2, ROWS, SEG), F32),
            pltpu.VMEM((4, 4, ROWS, SEG), BF16),
            pltpu.VMEM((ROWS, 128), F32),
            pltpu.VMEM((2, 4, ROWS, 128), F32),
            pltpu.VMEM((4, ROWS, 128), F32),
            pltpu.VMEM((4, ROWS, 128), F32),
            pltpu.VMEM((4, ROWS, HEAD), F32),
            pltpu.VMEM((32, HEAD, 128), F32),
            pltpu.VMEM((32, HEAD, 128), F32),
            pltpu.VMEM((4, SET, COLS), BF16),
            pltpu.VMEM((4, 2, 4, HEAD, 128), BF16),
            pltpu.VMEM((4, 2, 4, HEAD, 128), BF16),
            pltpu.VMEM((3, 2, 4, HEAD, 128), BF16),
            pltpu.VMEM((3, 2, 4, HEAD, 128), BF16),
            pltpu.VMEM((4, 2, HEAD, 128), BF16),
            pltpu.VMEM((4, 2, HEAD, 128), BF16),
            dma((2, 4, 2)), dma((2, 4, 2)),
            dma((2, 3)), dma((2, 3)),
            dma((3, 4)), dma((3, 4)),
            dma((4,)), dma((4,)),
            dma((5,)),
            dma((4, 2)), dma((4, 2)),
            dma((4,)), dma((4,)),
            dma((3,)), dma((3,)),
            dma((3,)), dma((3,)),
        ],
        compiler_params=pltpu.CompilerParams(
            collective_id=0, has_side_effects=True, vmem_limit_bytes=62 * 2**20
        ),
        name="attention_backward",
    )(queries, keys, values, output_gradient, span_order)
    parts = 2
    blocks = [pl.BlockSpec((x.shape[0] // parts, x.shape[1]), lambda n: (n, 0)) for x in results]
    return pl.pallas_call(
        hand_over,
        grid=(parts,),
        out_shape=[jax.ShapeDtypeStruct(x.shape, BF16) for x in results],
        in_specs=blocks,
        out_specs=blocks,
        compiler_params=pltpu.CompilerParams(vmem_limit_bytes=62 * 2**20),
        name="hand_over",
    )(*results)


def solution(mesh):
    rows = P(("outer", "inner"), None)
    return jax.shard_map(
        on_device,
        mesh=mesh,
        in_specs=(rows, rows, rows, rows, P()),
        out_specs=(rows, rows, rows),
        check_vma=False,
    )
```
